512 devices in a mesh: context: 64 (over z, y_hi, core), tensor: 8 (over y_lo, x).
Axes of the slice: x: 4, y: 8 (y_hi: 4, y_lo: 2; y = y_hi * 2 + y_lo), z: 8, core: 2. Of those that a mesh axis runs over, the one named last changes fastest.
Arguments:
- hidden_rows: bfloat16 [8192, 4096], P(('context', 'tensor')), may hold values from -6 to 6
- norm_gain: bfloat16 [4096], replicated, may hold values from 0.25 to 1.75
- w_qkv: bfloat16 [4096, 6144], P('context', 'tensor')
- w_out: bfloat16 [4096, 4096], P('tensor', 'context'), may hold values from -0.09375 to 0.09375
- doc_lengths: int32 [16], replicated, may hold values from 1 to 2048, 8192 in all
- span_order: int32 [128], replicated, may hold values from 0 to 127, each once
Outputs:
- attended: bfloat16 [8192, 4096], P(('context', 'tensor'))
The draws below stay inside these ranges and needn't reach their ends.
Inputs may be any that keep to these rules, and one draw needn't show every extreme that they name: `doc_lengths`: the lengths sum to 8192; the longest is exactly 2048. `span_order`: each initial span appears once.
All inputs are finite; a program needn't handle non-finite values.
Results may differ from the reference program's by a relative error of at most 0.02.
The reference program's roundings to bfloat16 on the way count: a program that leaves them out, or rounds other values in their place, can miss the bound.
Values may be sent and summed in bfloat16 or wider, within the bound.
A program may use at most 64 MiB of HBM per device.

```python
import math
import jax
import jax.numpy as jnp
import numpy as np
from jax import lax

D = 4096
HD = 128
QH_DEV = 4
NDOCS = 16
HEADS = 32
QKV_COLS = 768
TOKENS = 8192
SPAN = 64
MOST = 2048
N_CONTEXT = 64
N_TENSOR = 8


def draw_w_qkv(key, part):
    key = jax.random.fold_in(key, 7)
    base = jax.random.normal(key, (D, N_TENSOR * QKV_COLS), jnp.float32) / D ** 0.5
    return base.astype(jnp.bfloat16)


def levels(stream_key, extent, shards, low, high):
    def one(dim, parts):
        steps = jax.random.uniform(jax.random.fold_in(jax.random.fold_in(stream_key, 6), dim), (parts,), jnp.float32, low / len(shards), high / len(shards))
        return jnp.repeat(jnp.exp(steps), extent[dim] // parts).reshape((-1,) + (1,) * (len(extent) - dim - 1))

    factor_of = one(*shards[0])
    for cut in shards[1:]:
        factor_of = factor_of * one(*cut)
    return factor_of


def split_up(number_of, total, reach, lean):
    loads = [(1 << 20) // math.isqrt(standing ** lean) + 1 for standing in range(2, number_of + 1)]
    spare, holding = total - reach - (number_of - 1), [1] * (number_of - 1)
    while spare > 0:
        free = [i for i in range(number_of - 1) if holding[i] < reach]
        pool, budget = sum([loads[i] for i in free]), spare
        for i in free:
            addition = min(reach - holding[i], max(1, budget * loads[i] // pool), spare)
            holding[i] = holding[i] + addition
            spare = spare - addition
    return np.array([reach] + holding)


def ragged(stream_key, count, total, limit, skew):
    if count == 2:
        one = jax.random.randint(stream_key, (), max(1, total - limit), min(limit, total - 1) + 1)
        return jnp.stack([one, total - one])
    sizes = jnp.asarray(split_up(count, total, limit, skew), jnp.int32)
    couples = (count - 1) // 2
    giver, taker = sizes[1:1 + 2 * couples:2], sizes[2:2 + 2 * couples:2]
    slack = jnp.minimum(giver - 1, limit - taker)
    shifted = jax.random.randint(jax.random.fold_in(stream_key, 1), (couples,), 0, 1 << 20) % (slack + 1)
    sizes = sizes.at[1:1 + 2 * couples:2].set(giver - shifted).at[2:2 + 2 * couples:2].set(taker + shifted)
    return sizes[jax.random.permutation(jax.random.fold_in(stream_key, 2), count)]


def scatter_about(key, dims, deviation, most, pieces=(), held_as=jnp.bfloat16):
    result = jax.random.normal(key, dims, jnp.float32) * deviation
    if len(pieces) > 0:
        result = levels(key, dims, pieces, -0.22, 0.18) * result
    return jnp.clip(result, min=-most, max=most).astype(held_as)


def setup_inputs(seed: int = 0) -> dict:
    arg_keys = jax.random.split(jax.random.key(seed), 7)
    return {
        "hidden_rows": scatter_about(arg_keys[0], (TOKENS, D), 1.0, 6.0, ((0, 512),)),
        "norm_gain": jnp.clip(1.0 + 0.15 * jax.random.normal(arg_keys[1], (D,), jnp.float32), 0.25, 1.75).astype(jnp.bfloat16),
        "w_qkv": draw_w_qkv(jax.random.fold_in(arg_keys[6], 71), 0),
        "w_out": scatter_about(arg_keys[3], (HEADS * HD, D), (HEADS * HD) ** -0.5, 0.09375, ((0, 8), (1, 64))),
        "doc_lengths": ragged(arg_keys[4], NDOCS, TOKENS, MOST, 2).astype(jnp.int32),
        "span_order": jax.random.permutation(arg_keys[5], 2 * N_CONTEXT).astype(jnp.int32),
    }


rope_theta = 500000.0

def locate(layout_rows, span_order, doc_ends):
    span_index = layout_rows // SPAN
    matches = span_index[:, None] == jnp.arange(span_order.shape[0], dtype=jnp.int32)[None, :]
    source_span = lax.optimization_barrier(jnp.sum(jnp.where(matches, span_order[None, :], 0), axis=1)).astype(jnp.int32)
    initial = (source_span * SPAN + layout_rows % SPAN).astype(jnp.int32)
    document = lax.optimization_barrier(jnp.sum((initial[:, None] >= doc_ends[None, :]).astype(jnp.int32), axis=1)).astype(jnp.int32)
    doc_start = lax.optimization_barrier(jnp.max(jnp.where(doc_ends[None, :] <= initial[:, None], doc_ends[None, :], 0), axis=1))
    return (initial, document, (initial - doc_start).astype(jnp.int32))

def rotate(values, position):
    half = values.shape[-1] // 2
    freq = rope_theta ** (-(jnp.arange(half, dtype=jnp.float32) * 2.0 / values.shape[-1]))
    angle = position.astype(jnp.float32)[:, None, None] * freq[None, None, :]
    cosine = jnp.cos(angle)
    sine = jnp.sin(angle)
    first_half = values[..., :half]
    second_half = values[..., half:]
    return jnp.concatenate([first_half * cosine - second_half * sine, second_half * cosine + first_half * sine], axis=-1)

def reference(hidden_rows, norm_gain, w_qkv, w_out, doc_lengths, span_order):
    doc_ends = jnp.cumsum(doc_lengths).astype(jnp.int32)
    layout_rows = jnp.arange(TOKENS, dtype=jnp.int32)
    initial, document, position = locate(layout_rows, span_order, doc_ends)
    wide = hidden_rows.astype(jnp.float32)
    meansq = lax.optimization_barrier(jnp.mean(wide * wide, axis=-1, keepdims=True))
    normed = (wide * lax.rsqrt(meansq + 1e-05) * norm_gain.astype(jnp.float32)[None, :]).astype(jnp.bfloat16)
    qkv = jnp.dot(normed, w_qkv, preferred_element_type=jnp.float32).reshape(TOKENS, N_TENSOR, QKV_COLS)
    queries = qkv[:, :, :QH_DEV * HD].reshape(TOKENS, HEADS, HD)
    queries = rotate(queries, position).astype(jnp.bfloat16).transpose(1, 0, 2)
    keys = qkv[:, :, QH_DEV * HD:(QH_DEV + 1) * HD]
    keys = rotate(keys, position).astype(jnp.bfloat16).transpose(1, 0, 2)
    values = qkv[:, :, (QH_DEV + 1) * HD:].astype(jnp.bfloat16).transpose(1, 0, 2)
    allowed = (document[:, None] == document[None, :]) & (initial[None, :] <= initial[:, None])
    scale = 1.0 / HD ** 0.5

    def head_output(head):
        group = head // QH_DEV
        query_head = lax.dynamic_index_in_dim(queries, head, 0, keepdims=False)
        key_head = lax.dynamic_index_in_dim(keys, group, 0, keepdims=False)
        value_head = lax.dynamic_index_in_dim(values, group, 0, keepdims=False)
        scores = jnp.dot(query_head, key_head.T, preferred_element_type=jnp.float32) * scale
        scores = jnp.where(allowed, scores, -1e+30)
        top = lax.optimization_barrier(jnp.max(scores, axis=1, keepdims=True))
        expo = jnp.where(allowed, jnp.exp(scores - top), 0.0)
        totals = lax.optimization_barrier(jnp.sum(expo, axis=1, keepdims=True))
        weighted = jnp.dot(expo.astype(jnp.bfloat16), value_head, preferred_element_type=jnp.float32)
        return (weighted / totals).astype(jnp.bfloat16)
    mixed = lax.map(head_output, jnp.arange(HEADS, dtype=jnp.int32))
    mixed = mixed.transpose(1, 0, 2).reshape(TOKENS, HEADS * HD)
    return jnp.dot(mixed, w_out, preferred_element_type=jnp.float32).astype(jnp.bfloat16)
```

```python
import functools
import math

import jax
import jax.numpy as jnp
import numpy as np
from jax import lax
from jax.experimental import pallas as pl
from jax.experimental.pallas import tpu as pltpu
from jax.sharding import PartitionSpec as P

HD = 128
HEADS_HERE = 4
SPAN = 64
THETA = 500000.0
Y_HI = 4
CORES = 2
MASKED = -1e30
NT_DIMS = (((1,), (1,)), ((), ()))

W_IN, KV, W_OUT = 0, 1, 2


def kernel(
    NZ,
    NY,
    NT,
    span_ref,
    len_ref,
    hidden_ref,
    gain_ref,
    freq_ref,
    w_in_ref,
    w_out_ref,
    out_ref,
    w_in_own,
    w_in_sib,
    kv_own,
    kv_sib,
    w_out_own,
    w_out_sib,
    normed_ref,
    acc_ref,
    q_ref,
    kv_stage,
    o_ref,
    top_ref,
    sum_ref,
    mixed_ref,
    rs_send,
    rs_recv,
    own_recv,
    sib_recv,
    plane_send,
    ring_send,
    sib_send,
    norm_send,
    norm_recv,
    rs_send_sem,
    rs_recv_sem,
):
    PLANE = NY * CORES
    J = PLANE // 2
    rows, D = hidden_ref.shape
    tokens = rows * NT
    qcols = HEADS_HERE * HD
    half_k = J * w_in_ref.shape[0]
    half_c = J * w_out_ref.shape[0]

    ctx = lax.axis_index("context")
    t = lax.axis_index("tensor")
    z = ctx // PLANE
    y = (ctx % PLANE) // CORES
    core = ctx % CORES
    my_class = y // (NY // 2)
    slot = (y % (NY // 2)) * CORES + core
    step_z = 1 - 2 * core
    ahead = ((z + step_z + NZ) % NZ) * PLANE + y * CORES + core
    behind = ((z - step_z + NZ) % NZ) * PLANE + y * CORES + core
    sibling = z * PLANE + y * CORES + (1 - core)

    def device(c, u):
        return {"context": c, "tensor": u}

    own = (w_in_own, kv_own, w_out_own)
    sib = (w_in_sib, kv_sib, w_out_sib)

    barrier = pltpu.get_barrier_semaphore()
    for d in range(1, PLANE):
        c = z * PLANE + (ctx % PLANE + d) % PLANE
        pl.semaphore_signal(barrier, inc=1, device_id=device(c, t))
    for c in (ahead, behind):
        pl.semaphore_signal(barrier, inc=1, device_id=device(c, t))
    for d in range(1, NT):
        pl.semaphore_signal(barrier, inc=1, device_id=device(ctx, (t + d) % NT))

    wide = hidden_ref[...].astype(jnp.float32)
    meansq = jnp.mean(wide * wide, axis=-1, keepdims=True)
    normed = wide * lax.rsqrt(meansq + 1e-5) * gain_ref[...].astype(jnp.float32).reshape(1, D)
    normed_ref[t] = normed.astype(jnp.bfloat16)

    pl.semaphore_wait(barrier, PLANE - 1 + 2 + NT - 1)

    def plane_copy(g, src, d):
        c = z * PLANE + ((y + d) % NY) * CORES + my_class
        return pltpu.make_async_remote_copy(
            src_ref=src,
            dst_ref=own[g].at[0, slot],
            send_sem=plane_send.at[g, d],
            recv_sem=own_recv.at[g, 0, slot],
            device_id=device(c, t),
        )

    def plane_local(g, src):
        return pltpu.make_async_copy(src, own[g].at[0, slot], own_recv.at[g, 0, slot])

    def start_plane(g, src):
        @pl.when(core == my_class)
        def _():
            plane_local(g, src).start()

        @pl.when(core != my_class)
        def _():
            plane_copy(g, src, 0).start()

        for d in range(1, NY):
            plane_copy(g, src, d).start()

    def finish_plane(g, src):
        @pl.when(core != my_class)
        def _():
            plane_copy(g, src, 0).wait_send()

        for d in range(1, NY):
            plane_copy(g, src, d).wait_send()

    def pass_on(g, s):
        for j in range(J):
            unit = own[g].at[s, j]
            pltpu.make_async_copy(unit, unit, own_recv.at[g, s, j]).wait()

            @pl.when(s < NZ - 1)
            def _():
                pltpu.make_async_remote_copy(
                    src_ref=unit,
                    dst_ref=own[g].at[s + 1, j],
                    send_sem=ring_send.at[g],
                    recv_sem=own_recv.at[g, s + 1, j],
                    device_id=device(ahead, t),
                ).start()

            pltpu.make_async_remote_copy(
                src_ref=unit,
                dst_ref=sib[g].at[s, j],
                send_sem=sib_send.at[g],
                recv_sem=sib_recv.at[g, s],
                device_id=device(sibling, t),
            ).start()

    def wait_sibling(g, s):
        whole = sib[g].at[s]
        pltpu.make_async_copy(whole, whole, sib_recv.at[g, s]).wait()

    def finish_gather(g):
        sent = own[g].at[pl.ds(0, NZ - 1)]
        pltpu.make_async_copy(sent, sent, ring_send.at[g]).wait()
        pltpu.make_async_copy(sib[g], sib[g], sib_send.at[g]).wait()

    def own_half(s):
        return ((z - step_z * s + NZ) % NZ) * 2 + core

    def sib_half(s):
        return ((z + step_z * s + NZ) % NZ) * 2 + 1 - core

    start_plane(W_IN, w_in_ref)

    def norm_copy(d):
        return pltpu.make_async_remote_copy(
            src_ref=normed_ref.at[t],
            dst_ref=normed_ref.at[t],
            send_sem=norm_send.at[d - 1],
            recv_sem=norm_recv.at[t],
            device_id=device(ctx, (t + d) % NT),
        )

    for d in range(1, NT):
        norm_copy(d).start()

    start_plane(W_OUT, w_out_ref)

    acc_ref[...] = jnp.zeros_like(acc_ref)
    for d in range(1, NT):
        block = normed_ref.at[(t + NT - d) % NT]
        pltpu.make_async_copy(block, block, norm_recv.at[(t + NT - d) % NT]).wait()

    def project(s):
        wait_sibling(W_IN, s)
        total = acc_ref[...]
        for half, ref in ((own_half(s), w_in_own), (sib_half(s), w_in_sib)):
            cols = pl.ds(pl.multiple_of(half * half_k, half_k), half_k)
            left = normed_ref[:, :, cols].reshape(tokens, half_k)
            right = ref[s].reshape(half_k, ref.shape[-1])
            total += jnp.dot(left, right, preferred_element_type=jnp.float32)
        acc_ref[...] = total

    def project_step(s, carry):
        pass_on(W_IN, s)

        @pl.when(s > 0)
        def _():
            project(s - 1)

        return carry

    lax.fori_loop(0, NZ, project_step, 0)
    pass_on(W_OUT, 0)
    project(NZ - 1)

    row = lax.broadcasted_iota(jnp.int32, (tokens, 1), 0)
    source = jnp.zeros_like(row)
    for a in range(tokens // SPAN):
        source = jnp.where(row // SPAN == a, span_ref[ctx * (tokens // SPAN) + a], source)
    orig = source * SPAN + row % SPAN
    start = jnp.zeros_like(orig)
    end = jnp.int32(0)
    for i in range(len_ref.shape[0]):
        end = end + len_ref[i]
        start = jnp.where(end <= orig, jnp.maximum(start, end), start)

    angle = (orig - start).astype(jnp.float32) * freq_ref[...]
    lane = lax.broadcasted_iota(jnp.int32, (tokens, HD), 1)
    cosine = jnp.cos(angle)
    sine = jnp.where(lane < HD // 2, -jnp.sin(angle), jnp.sin(angle))

    def rotate(x):
        return (x * cosine + pltpu.roll(x, HD // 2, 1) * sine).astype(jnp.bfloat16)

    kv_stage[:, :HD] = rotate(acc_ref[:, qcols : qcols + HD])
    kv_stage[:, HD:] = acc_ref[:, qcols + HD :].astype(jnp.bfloat16)
    start_plane(KV, kv_stage)
    for h in range(HEADS_HERE):
        q_ref[h * tokens : (h + 1) * tokens, :] = rotate(acc_ref[:, h * HD : (h + 1) * HD])

    top_ref[...] = jnp.full_like(top_ref, MASKED)
    sum_ref[...] = jnp.zeros_like(sum_ref)
    o_ref[...] = jnp.zeros_like(o_ref)
    keys = J * tokens
    scale = math.log2(math.e) / HD**0.5

    def attend_half(half, ref, s):
        lane = lax.broadcasted_iota(jnp.int32, (1, keys), 1)
        key_source = jnp.zeros_like(lane)
        spans = keys // SPAN
        for a in range(spans):
            key_source = jnp.where(lane // SPAN == a, span_ref[half * spans + a], key_source)
        key_orig = key_source * SPAN + lane % SPAN
        allowed = (start <= key_orig) & (key_orig <= orig)
        k = ref[s, :, :, :HD].reshape(keys, HD)
        v = ref[s, :, :, HD:].reshape(keys, HD)
        for h in range(HEADS_HERE):
            at = pl.ds(h * tokens, tokens)
            scores = lax.dot_general(q_ref[at, :], k, NT_DIMS, preferred_element_type=jnp.float32)
            scores = jnp.where(allowed, scores, MASKED)
            old = top_ref[at, :]
            new = jnp.maximum(old, jnp.max(scores, axis=1, keepdims=True))
            expo = jnp.exp2((scores - new) * scale)
            fade = jnp.exp2((old - new) * scale)
            top_ref[at, :] = new
            sum_ref[at, :] = sum_ref[at, :] * fade + jnp.sum(expo, axis=1, keepdims=True)
            o_ref[at, :] = o_ref[at, :] * fade + jnp.dot(
                expo.astype(jnp.bfloat16), v, preferred_element_type=jnp.float32
            )

    def attend(s):
        attend_half(own_half(s), kv_own, s)
        wait_sibling(KV, s)
        attend_half(sib_half(s), kv_sib, s)

    def attend_step(s, carry):
        pass_on(KV, s)

        @pl.when(s > 0)
        def _():
            attend(s - 1)

        return carry

    lax.fori_loop(0, NZ, attend_step, 0)
    pass_on(W_OUT, 1)
    attend(NZ - 1)
    for h in range(HEADS_HERE):
        at = pl.ds(h * tokens, tokens)
        mixed_ref[:, h * HD : (h + 1) * HD] = (o_ref[at, :] / sum_ref[at, :]).astype(jnp.bfloat16)

    def rs_copy(s, d):
        u = (t + d) % NT
        return pltpu.make_async_remote_copy(
            src_ref=rs_send.at[s, u],
            dst_ref=rs_recv.at[s, d - 1],
            send_sem=rs_send_sem,
            recv_sem=rs_recv_sem.at[s],
            device_id=device(ctx, u),
        )

    def share(s):
        wait_sibling(W_OUT, s)
        for i, ref in enumerate((w_out_own, w_out_sib)):
            right = ref[s].reshape(half_c, ref.shape[-1])
            part = lax.dot_general(mixed_ref[...], right, NT_DIMS, preferred_element_type=jnp.float32)
            part = part.astype(jnp.bfloat16).reshape(NT, rows, half_c)
            rs_send[s, :, :, i * half_c : (i + 1) * half_c] = part
        for d in range(1, NT):
            rs_copy(s, d).start()

    def share_step(s, carry):
        @pl.when(s > 1)
        def _():
            pass_on(W_OUT, s)

        share(s - 1)
        return carry

    lax.fori_loop(1, NZ, share_step, 0)
    share(NZ - 1)

    def add_up(s, carry):
        whole = rs_recv.at[s]
        pltpu.make_async_copy(whole, whole, rs_recv_sem.at[s]).wait()
        total = rs_send[s, t].astype(jnp.float32)
        for d in range(1, NT):
            total += rs_recv[s, d - 1].astype(jnp.float32)
        total = total.astype(jnp.bfloat16)
        for i, half in enumerate((own_half(s), sib_half(s))):
            cols = pl.ds(pl.multiple_of(half * half_c, half_c), half_c)
            out_ref[:, cols] = total[:, i * half_c : (i + 1) * half_c]
        return carry

    lax.fori_loop(0, NZ, add_up, 0)

    finish_plane(W_IN, w_in_ref)
    finish_plane(W_OUT, w_out_ref)
    finish_plane(KV, kv_stage)
    for g in (W_IN, KV, W_OUT):
        finish_gather(g)
    for d in range(1, NT):
        norm_copy(d).wait_send()
    pltpu.make_async_copy(rs_recv, rs_recv, rs_send_sem).wait()


def per_device(NC, NT, NY, hidden_rows, norm_gain, w_qkv, w_out, doc_lengths, span_order):
    J = NY * CORES // 2
    NZ = NC // (NY * CORES)
    rows, D = hidden_rows.shape
    tokens = rows * NT
    k_rows, in_cols = w_qkv.shape
    out_rows, c_cols = w_out.shape
    qcols = HEADS_HERE * HD
    freq = THETA ** (-(np.arange(HD // 2, dtype=np.float64) * 2.0 / HD))
    freq = jnp.asarray(np.tile(freq, 2)[None, :].astype(np.float32))
    bf16, f32 = jnp.bfloat16, jnp.float32
    vmem = pl.BlockSpec(memory_space=pltpu.VMEM)
    smem = pl.BlockSpec(memory_space=pltpu.SMEM)
    anywhere = pl.BlockSpec(memory_space=pl.ANY)
    DMA = pltpu.SemaphoreType.DMA
    return pl.pallas_call(
        functools.partial(kernel, NZ, NY, NT),
        out_shape=jax.ShapeDtypeStruct((rows, D), bf16),
        in_specs=[smem, smem, vmem, vmem, vmem, anywhere, anywhere],
        out_specs=vmem,
        scratch_shapes=[
            pltpu.VMEM((NZ, J, k_rows, in_cols), bf16),
            pltpu.VMEM((NZ, J, k_rows, in_cols), bf16),
            pltpu.VMEM((NZ, J, tokens, 2 * HD), bf16),
            pltpu.VMEM((NZ, J, tokens, 2 * HD), bf16),
            pltpu.VMEM((NZ, J, c_cols, out_rows), bf16),
            pltpu.VMEM((NZ, J, c_cols, out_rows), bf16),
            pltpu.VMEM((NT, rows, D), bf16),
            pltpu.VMEM((tokens, in_cols), f32),
            pltpu.VMEM((HEADS_HERE * tokens, HD), bf16),
            pltpu.VMEM((tokens, 2 * HD), bf16),
            pltpu.VMEM((HEADS_HERE * tokens, HD), f32),
            pltpu.VMEM((HEADS_HERE * tokens, 1), f32),
            pltpu.VMEM((HEADS_HERE * tokens, 1), f32),
            pltpu.VMEM((tokens, qcols), bf16),
            pltpu.VMEM((NZ, NT, rows, 2 * J * c_cols), bf16),
            pltpu.VMEM((NZ, NT - 1, rows, 2 * J * c_cols), bf16),
            DMA((3, NZ, J)),
            DMA((3, NZ)),
            DMA((3, NY)),
            DMA((3,)),
            DMA((3,)),
            DMA((NT - 1,)),
            DMA((NT,)),
            DMA,
            DMA((NZ,)),
        ],
        compiler_params=pltpu.CompilerParams(
            collective_id=0, has_side_effects=True, vmem_limit_bytes=48 * 2**20
        ),
        cost_estimate=pl.CostEstimate(
            flops=2 * tokens * (D * in_cols + qcols * 2 * NC * tokens + out_rows * D),
            bytes_accessed=4 * rows * D,
            transcendentals=HEADS_HERE * tokens * tokens * NC,
        ),
    )(span_order, doc_lengths, hidden_rows, norm_gain, freq, w_qkv, w_out.T)


def build(mesh, NY):
    placed = (
        P(("context", "tensor"), None),
        P(),
        P("context", "tensor"),
        P("tensor", "context"),
        P(),
        P(),
    )
    return jax.shard_map(
        functools.partial(per_device, mesh.shape["context"], mesh.shape["tensor"], NY),
        mesh=mesh,
        in_specs=placed,
        out_specs=P(("context", "tensor"), None),
        check_vma=False,
    )


def solution(mesh):
    return build(mesh, Y_HI)
```

```python
import functools
import math

import jax
import jax.numpy as jnp
import numpy as np
from jax import lax
from jax.experimental import pallas as pl
from jax.experimental.pallas import tpu as pltpu
from jax.sharding import PartitionSpec as P

HD = 128
HEADS_HERE = 4
SPAN = 64
THETA = 500000.0
Y_HI = 4
CORES = 2
MASKED = -1e30
NT_DIMS = (((1,), (1,)), ((), ()))

W_IN, KV, W_OUT = 0, 1, 2


def kernel(
    NZ,
    NY,
    NT,
    span_ref,
    len_ref,
    hidden_hbm,
    gain_hbm,
    freq_hbm,
    w_in_ref,
    w_out_ref,
    out_ref,
    hidden_ref,
    gain_ref,
    freq_ref,
    cos_ref,
    sin_ref,
    w_in_own,
    w_in_sib,
    kv_own,
    kv_sib,
    w_out_own,
    w_out_sib,
    normed_ref,
    acc_ref,
    q_ref,
    kv_stage,
    o_ref,
    top_ref,
    sum_ref,
    mixed_ref,
    rs_send,
    rs_recv,
    own_recv,
    sib_recv,
    plane_send,
    ring_send,
    sib_send,
    norm_send,
    norm_recv,
    rs_send_sem,
    rs_recv_sem,
    load_sem,
):
    PLANE = NY * CORES
    J = PLANE // 2
    rows, D = hidden_ref.shape
    tokens = rows * NT
    qcols = HEADS_HERE * HD
    piece_k = D // NZ
    half_cols = w_in_ref.shape[1] // 2
    half_c = J * w_out_ref.shape[0]
    order = ((0, 0), (1, 1), (3, 1), (2, 1)) if NY == 4 else ((0, 0), (1, 1))
    H = NZ // 2

    ctx = lax.axis_index("context")
    t = lax.axis_index("tensor")
    z = ctx // PLANE
    y = (ctx % PLANE) // CORES
    core = ctx % CORES
    my_class = y // (NY // 2)
    slot = (y % (NY // 2)) * CORES + core
    above = ((z + 1) % NZ) * PLANE + y * CORES + core
    below = ((z + NZ - 1) % NZ) * PLANE + y * CORES + core
    sibling = z * PLANE + y * CORES + (1 - core)

    def device(c, u):
        return {"context": c, "tensor": u}

    loads = [
        pltpu.make_async_copy(src, dst, load_sem.at[i])
        for i, (src, dst) in enumerate(
            ((hidden_hbm, hidden_ref), (gain_hbm, gain_ref), (freq_hbm, freq_ref))
        )
    ]
    for load in loads:
        load.start()

    own = (w_in_own, kv_own, w_out_own)
    sib = (w_in_sib, kv_sib, w_out_sib)

    barrier = pltpu.get_barrier_semaphore()
    for d in range(1, PLANE):
        c = z * PLANE + (ctx % PLANE + d) % PLANE
        pl.semaphore_signal(barrier, inc=1, device_id=device(c, t))
    for c in (above, below):
        pl.semaphore_signal(barrier, inc=1, device_id=device(c, t))
    for d in range(1, NT):
        pl.semaphore_signal(barrier, inc=1, device_id=device(ctx, (t + d) % NT))

    pl.semaphore_wait(barrier, PLANE - 1 + 2 + NT - 1)

    def plane_copies(g, src):
        copies = []
        if g == W_OUT:
            for d, _ in order:
                copies.append((d, my_class, src, own[g].at[0, slot], own_recv.at[g, 0, slot]))
        else:
            for d, _ in order:
                for c in range(CORES):
                    if g == W_IN:
                        half = src.at[:, c * half_cols : (c + 1) * half_cols]
                    else:
                        half = src.at[c * (tokens // 2) : (c + 1) * (tokens // 2), :]
                    n = half.shape[0]
                    part = pl.ds(pl.multiple_of(core * n, n), n)
                    copies.append((d, c, half, own[g].at[0, y, part], own_recv.at[g, 0, y]))
        for i, (d, c, half, dst, sem) in enumerate(copies):
            chip = z * PLANE + ((y + d) % NY) * CORES
            remote = functools.partial(
                pltpu.make_async_remote_copy,
                src_ref=half,
                dst_ref=dst,
                send_sem=plane_send.at[g, i],
                recv_sem=sem,
                device_id=device(chip + c, t),
            )
            local = functools.partial(pltpu.make_async_copy, half, dst, sem)
            yield d, c, remote, local

    def start_plane(g, src):
        for d, c, remote, local in plane_copies(g, src):
            if d == 0:
                pl.when(core == c)(lambda: local().start())
                pl.when(core != c)(lambda: remote().start())
            else:
                remote().start()

    def finish_plane(g, src):
        for d, c, remote, local in plane_copies(g, src):
            if d == 0:
                pl.when(core != c)(lambda: remote().wait_send())
            else:
                remote().wait_send()

    def take(g, q, j):
        unit = own[g].at[q, j]
        pltpu.make_async_copy(unit, unit, own_recv.at[g, q, j]).wait()
        pltpu.make_async_remote_copy(
            src_ref=unit,
            dst_ref=sib[g].at[q, j],
            send_sem=sib_send.at[g],
            recv_sem=sib_recv.at[g, q],
            device_id=device(sibling, t),
        ).start()

    def forward(g, q, j, to, q_there):
        pltpu.make_async_remote_copy(
            src_ref=own[g].at[q, j],
            dst_ref=own[g].at[q_there, j],
            send_sem=ring_send.at[g],
            recv_sem=own_recv.at[g, q_there, j],
            device_id=device(to, t),
        ).start()

    def pass_unit(g, s, j, from_below):
        up_last = H if from_below else H - 1
        down_last = H - 1 if from_below else H

        @pl.when(s == 0)
        def _():
            take(g, 0, j)
            if up_last > 0:
                forward(g, 0, j, above, 1)
            if down_last > 0:
                forward(g, 0, j, below, NZ - 1)

        @pl.when((s > 0) & (s < H))
        def _():
            take(g, s, j)
            pl.when(s < up_last)(lambda: forward(g, s, j, above, s + 1))
            take(g, NZ - s, j)
            pl.when(s < down_last)(lambda: forward(g, NZ - s, j, below, NZ - s - 1))

        @pl.when(s == H)
        def _():
            take(g, H, j)

    def pass_on(g, s):
        for j in range(J):
            pass_unit(g, s, j, j < J // 2)

    def pass_skewed(g, m):
        for i, (d, late) in enumerate(order):
            s = m - late

            @pl.when((s >= 0) & (s <= H))
            def _():
                pass_unit(g, s, (y + d) % NY, i < NY // 2)

    def for_slots(s, act):
        act(s)
        pl.when((s > 0) & (s < H))(lambda: act(NZ - s))

    def wait_sibling(g, q):
        whole = sib[g].at[q]
        pltpu.make_async_copy(whole, whole, sib_recv.at[g, q]).wait()

    def finish_gather(g):
        sent = own[g].at[pl.ds(0, NZ - 1)]
        pltpu.make_async_copy(sent, sent, ring_send.at[g]).wait()
        pltpu.make_async_copy(sib[g], sib[g], sib_send.at[g]).wait()

    def source_z(q):
        return (z + NZ - q) % NZ

    start_plane(W_IN, w_in_ref)

    for load in loads:
        load.wait()
    wide = hidden_ref[...].astype(jnp.float32)
    meansq = jnp.mean(wide * wide, axis=-1, keepdims=True)
    gain = gain_ref[...].astype(jnp.float32).reshape(1, D)
    normed_ref[t] = (wide * lax.rsqrt(meansq + 1e-5) * gain).astype(jnp.bfloat16)

    def norm_copy(d):
        return pltpu.make_async_remote_copy(
            src_ref=normed_ref.at[t],
            dst_ref=normed_ref.at[t],
            send_sem=norm_send.at[d - 1],
            recv_sem=norm_recv.at[t],
            device_id=device(ctx, (t + d) % NT),
        )

    for d in range(1, NT):
        norm_copy(d).start()

    start_plane(W_OUT, w_out_ref)

    row = lax.broadcasted_iota(jnp.int32, (tokens, 1), 0)
    source = jnp.zeros_like(row)
    for a in range(tokens // SPAN):
        source = jnp.where(row // SPAN == a, span_ref[ctx * (tokens // SPAN) + a], source)
    orig = source * SPAN + row % SPAN
    start = jnp.zeros_like(orig)
    end = jnp.int32(0)
    for i in range(len_ref.shape[0]):
        end = end + len_ref[i]
        start = jnp.where(end <= orig, jnp.maximum(start, end), start)

    angle = (orig - start).astype(jnp.float32) * freq_ref[...]
    lane = lax.broadcasted_iota(jnp.int32, (tokens, HD), 1)
    cos_ref[...] = jnp.cos(angle)
    sine = jnp.sin(angle)
    sin_ref[...] = jnp.where(lane < HD // 2, -sine, sine)

    acc_ref[...] = jnp.zeros_like(acc_ref)
    top_ref[...] = jnp.full_like(top_ref, MASKED)
    sum_ref[...] = jnp.zeros_like(sum_ref)
    o_ref[...] = jnp.zeros_like(o_ref)

    def project(q):
        wait_sibling(W_IN, q)
        cols = pl.ds(pl.multiple_of(source_z(q) * piece_k, piece_k), piece_k)
        left = normed_ref[:, :, cols].reshape(tokens, piece_k)
        for c, ref in ((core, w_in_own), (1 - core, w_in_sib)):
            right = ref[q].reshape(piece_k, half_cols)
            acc_ref[c] += jnp.dot(left, right, preferred_element_type=jnp.float32)

    def project_step(m, carry):
        pass_skewed(W_IN, m)

        @pl.when(m == H)
        def _():
            pass_on(W_OUT, 0)

        @pl.when(m == 2)
        def _():
            for d in range(1, NT):
                other = (t + NT - d) % NT
                block = normed_ref.at[other]
                pltpu.make_async_copy(block, block, norm_recv.at[other]).wait()

        @pl.when(m >= 2)
        def _():
            for_slots(m - 2, project)

        return carry

    lax.fori_loop(0, H + 2, project_step, 0)
    project(H)

    scale = math.log2(math.e) / HD**0.5
    cosine = cos_ref[...]
    sine = sin_ref[...]

    def rotate(x):
        return x * cosine + pltpu.roll(x, HD // 2, 1) * sine

    def columns(i):
        per = half_cols // HD
        return acc_ref[i // per, :, (i % per) * HD : (i % per + 1) * HD]

    kv_stage[:, :HD] = rotate(columns(HEADS_HERE)).astype(jnp.bfloat16)
    kv_stage[:, HD:] = columns(HEADS_HERE + 1).astype(jnp.bfloat16)
    start_plane(KV, kv_stage)
    for h in range(HEADS_HERE):
        q_ref[h * tokens : (h + 1) * tokens, :] = (rotate(columns(h)) * scale).astype(jnp.bfloat16)

    keys = J * tokens
    spans = keys // SPAN

    def attend_half(at, c, ref, q):
        lane = lax.broadcasted_iota(jnp.int32, (1, keys), 1)
        key_source = jnp.zeros_like(lane)
        for a in range(spans):
            held = span_ref[2 * (at * spans + a) + c]
            key_source = jnp.where(lane // SPAN == a, held, key_source)
        key_orig = key_source * SPAN + lane % SPAN
        allowed = (start <= key_orig) & (key_orig <= orig)
        cap = jnp.where(allowed, 3e38, MASKED)
        k = ref[q, :, :, :HD].reshape(keys, HD)
        v = ref[q, :, :, HD:].reshape(keys, HD)
        scores = lax.dot_general(q_ref[...], k, NT_DIMS, preferred_element_type=jnp.float32)
        weights = []
        for h in range(HEADS_HERE):
            rows_h = slice(h * tokens, (h + 1) * tokens)
            mine = jnp.minimum(scores[rows_h], cap)
            old = top_ref[rows_h, :]
            new = jnp.maximum(old, jnp.max(mine, axis=1, keepdims=True))
            fade = jnp.exp2(old - new)
            top_ref[rows_h, :] = new
            expo = [jnp.exp2(mine[:, i : i + HD] - new) for i in range(0, keys, HD)]
            sum_ref[rows_h, :] = sum_ref[rows_h, :] * fade + functools.reduce(jnp.add, expo)
            o_ref[rows_h, :] = o_ref[rows_h, :] * fade
            weights.append(jnp.concatenate([e.astype(jnp.bfloat16) for e in expo], axis=1))
        weights = jnp.concatenate(weights, axis=0)
        o_ref[...] += jnp.dot(weights, v, preferred_element_type=jnp.float32)

    def attend(q):
        attend_half(source_z(q), core, kv_own, q)
        wait_sibling(KV, q)
        attend_half(source_z(q), 1 - core, kv_sib, q)

    def attend_step(m, carry):
        pass_skewed(KV, m)

        @pl.when(m == 1)
        def _():
            pass_on(W_OUT, 1)

        @pl.when(m == H)
        def _():
            pass_on(W_OUT, min(2, H))

        @pl.when(m >= 2)
        def _():
            for_slots(m - 2, attend)

        return carry

    lax.fori_loop(0, H + 2, attend_step, 0)
    attend(H)
    for h in range(HEADS_HERE):
        at = pl.ds(h * tokens, tokens)
        mixed_ref[:, h * HD : (h + 1) * HD] = (
            o_ref[at, :] / jnp.sum(sum_ref[at, :], axis=1, keepdims=True)
        ).astype(jnp.bfloat16)

    def rs_copy(q, d):
        u = (t + d) % NT
        return pltpu.make_async_remote_copy(
            src_ref=rs_send.at[q, u],
            dst_ref=rs_recv.at[q, d - 1],
            send_sem=rs_send_sem,
            recv_sem=rs_recv_sem.at[q],
            device_id=device(ctx, u),
        )

    def share(q):
        wait_sibling(W_OUT, q)
        for i, ref in enumerate((w_out_own, w_out_sib)):
            right = ref[q].reshape(half_c, ref.shape[-1])
            part = lax.dot_general(mixed_ref[...], right, NT_DIMS, preferred_element_type=jnp.float32)
            part = part.astype(jnp.bfloat16).reshape(NT, rows, half_c)
            rs_send[q, :, :, i * half_c : (i + 1) * half_c] = part
        for d in range(1, NT):
            rs_copy(q, d).start()

    def add_up(q):
        whole = rs_recv.at[q]
        pltpu.make_async_copy(whole, whole, rs_recv_sem.at[q]).wait()
        total = rs_send[q, t].astype(jnp.float32)
        for d in range(1, NT):
            total += rs_recv[q, d - 1].astype(jnp.float32)
        total = total.astype(jnp.bfloat16)
        for i, c in enumerate((core, 1 - core)):
            cols = pl.ds(pl.multiple_of((source_z(q) * 2 + c) * half_c, half_c), half_c)
            out_ref[:, cols] = total[:, i * half_c : (i + 1) * half_c]

    def share_step(s, carry):
        @pl.when(s > 2)
        def _():
            pass_on(W_OUT, s)

        for_slots(s - 1, share)

        @pl.when(s > 2)
        def _():
            for_slots(s - 3, add_up)

        return carry

    lax.fori_loop(1, H + 1, share_step, 0)
    share(H)

    def add_step(s, carry):
        for_slots(s, add_up)
        return carry

    lax.fori_loop(max(H - 2, 0), H + 1, add_step, 0)

    finish_plane(W_IN, w_in_ref)
    finish_plane(W_OUT, w_out_ref)
    finish_plane(KV, kv_stage)
    for g in (W_IN, KV, W_OUT):
        finish_gather(g)
    for d in range(1, NT):
        norm_copy(d).wait_send()
    pltpu.make_async_copy(rs_recv, rs_recv, rs_send_sem).wait()


def per_device(NC, NT, NY, hidden_rows, norm_gain, w_qkv, w_out, doc_lengths, span_order):
    J = NY * CORES // 2
    NZ = NC // (NY * CORES)
    rows, D = hidden_rows.shape
    tokens = rows * NT
    k_rows, in_cols = w_qkv.shape
    out_rows, c_cols = w_out.shape
    qcols = HEADS_HERE * HD
    freq = THETA ** (-(np.arange(HD // 2, dtype=np.float64) * 2.0 / HD))
    freq = jnp.asarray(np.tile(freq, 2)[None, :].astype(np.float32))
    bf16, f32 = jnp.bfloat16, jnp.float32
    vmem = pl.BlockSpec(memory_space=pltpu.VMEM)
    smem = pl.BlockSpec(memory_space=pltpu.SMEM)
    hbm = pl.BlockSpec(memory_space=pltpu.HBM)
    DMA = pltpu.SemaphoreType.DMA
    return pl.pallas_call(
        functools.partial(kernel, NZ, NY, NT),
        out_shape=jax.ShapeDtypeStruct((rows, D), bf16),
        in_specs=[smem, smem, hbm, hbm, hbm, hbm, hbm],
        out_specs=vmem,
        scratch_shapes=[
            pltpu.VMEM((rows, D), bf16),
            pltpu.VMEM((D,), bf16),
            pltpu.VMEM((1, HD), f32),
            pltpu.VMEM((tokens, HD), f32),
            pltpu.VMEM((tokens, HD), f32),
            pltpu.VMEM((NZ, NY, CORES * k_rows, in_cols // 2), bf16),
            pltpu.VMEM((NZ, NY, CORES * k_rows, in_cols // 2), bf16),
            pltpu.VMEM((NZ, NY, tokens, 2 * HD), bf16),
            pltpu.VMEM((NZ, NY, tokens, 2 * HD), bf16),
            pltpu.VMEM((NZ, J, c_cols, out_rows), bf16),
            pltpu.VMEM((NZ, J, c_cols, out_rows), bf16),
            pltpu.VMEM((NT, rows, D), bf16),
            pltpu.VMEM((CORES, tokens, in_cols // 2), f32),
            pltpu.VMEM((HEADS_HERE * tokens, HD), bf16),
            pltpu.VMEM((tokens, 2 * HD), bf16),
            pltpu.VMEM((HEADS_HERE * tokens, HD), f32),
            pltpu.VMEM((HEADS_HERE * tokens, HD), f32),
            pltpu.VMEM((HEADS_HERE * tokens, HD), f32),
            pltpu.VMEM((tokens, qcols), bf16),
            pltpu.VMEM((NZ, NT, rows, 2 * J * c_cols), bf16),
            pltpu.VMEM((NZ, NT - 1, rows, 2 * J * c_cols), bf16),
            DMA((3, NZ, J)),
            DMA((3, NZ)),
            DMA((3, 2 * NY)),
            DMA((3,)),
            DMA((3,)),
            DMA((NT - 1,)),
            DMA((NT,)),
            DMA,
            DMA((NZ,)),
            DMA((3,)),
        ],
        compiler_params=pltpu.CompilerParams(
            collective_id=0, has_side_effects=True, vmem_limit_bytes=62 * 2**20
        ),
        cost_estimate=pl.CostEstimate(
            flops=2 * tokens * (D * in_cols + qcols * 2 * NC * tokens + out_rows * D),
            bytes_accessed=4 * rows * D,
            transcendentals=HEADS_HERE * tokens * tokens * NC,
        ),
    )(span_order, doc_lengths, hidden_rows, norm_gain, freq, w_qkv, w_out.T)


def build(mesh, NY):
    placed = (
        P(("context", "tensor"), None),
        P(),
        P("context", "tensor"),
        P("tensor", "context"),
        P(),
        P(),
    )
    return jax.shard_map(
        functools.partial(per_device, mesh.shape["context"], mesh.shape["tensor"], NY),
        mesh=mesh,
        in_specs=placed,
        out_specs=P(("context", "tensor"), None),
        check_vma=False,
    )


def solution(mesh):
    return build(mesh, Y_HI)
```

```python
import functools
import math

import jax
import jax.numpy as jnp
import numpy as np
from jax import lax
from jax.experimental import pallas as pl
from jax.experimental.pallas import tpu as pltpu
from jax.sharding import PartitionSpec as P

HD = 128
HEADS_HERE = 4
SPAN = 64
THETA = 500000.0
Y_HI = 4
CORES = 2
MASKED = -1e30
NT_DIMS = (((1,), (1,)), ((), ()))

W_KV, W_Q, KV, W_OUT = 0, 1, 2, 3
GATHERS = 4


def kernel(
    NZ,
    NY,
    NT,
    span_ref,
    len_ref,
    hidden_hbm,
    gain_hbm,
    freq_hbm,
    w_in_ref,
    w_out_ref,
    out_ref,
    hidden_ref,
    gain_ref,
    freq_ref,
    cos_ref,
    sin_ref,
    w_kv_own,
    w_kv_sib,
    w_q_own,
    w_q_sib,
    kv_own,
    kv_sib,
    w_out_own,
    w_out_sib,
    normed_ref,
    acc_kv,
    acc_q,
    q_ref,
    kv_stage,
    o_ref,
    top_ref,
    sum_ref,
    mixed_ref,
    rs_send,
    rs_recv,
    own_recv,
    sib_recv,
    plane_send,
    ring_send,
    sib_send,
    norm_send,
    norm_recv,
    rs_send_sem,
    rs_recv_sem,
    load_sem,
):
    PLANE = NY * CORES
    J = PLANE // 2
    rows, D = hidden_ref.shape
    tokens = rows * NT
    qcols = HEADS_HERE * HD
    piece_k = D // NZ
    half_c = J * w_out_ref.shape[0]
    order = (0, 1, 3, 2) if NY == 4 else (0, 1)
    H = NZ // 2

    ctx = lax.axis_index("context")
    t = lax.axis_index("tensor")
    z = ctx // PLANE
    y = (ctx % PLANE) // CORES
    core = ctx % CORES
    my_class = y // (NY // 2)
    slot = (y % (NY // 2)) * CORES + core
    above = ((z + 1) % NZ) * PLANE + y * CORES + core
    below = ((z + NZ - 1) % NZ) * PLANE + y * CORES + core
    sibling = z * PLANE + y * CORES + (1 - core)

    def device(c, u):
        return {"context": c, "tensor": u}

    loads = [
        pltpu.make_async_copy(src, dst, load_sem.at[i])
        for i, (src, dst) in enumerate(
            ((hidden_hbm, hidden_ref), (gain_hbm, gain_ref), (freq_hbm, freq_ref))
        )
    ]
    for load in loads:
        load.start()

    own = (w_kv_own, w_q_own, kv_own, w_out_own)
    sib = (w_kv_sib, w_q_sib, kv_sib, w_out_sib)

    barrier = pltpu.get_barrier_semaphore()
    for d in range(1, PLANE):
        c = z * PLANE + (ctx % PLANE + d) % PLANE
        pl.semaphore_signal(barrier, inc=1, device_id=device(c, t))
    for c in (above, below):
        pl.semaphore_signal(barrier, inc=1, device_id=device(c, t))
    for d in range(1, NT):
        pl.semaphore_signal(barrier, inc=1, device_id=device(ctx, (t + d) % NT))

    pl.semaphore_wait(barrier, PLANE - 1 + 2 + NT - 1)

    def plane_copies(g, src):
        copies = []
        if g == W_OUT:
            for d in order:
                copies.append((d, my_class, src, own[g].at[0, slot], own_recv.at[g, 0, slot]))
        else:
            for d in order:
                for c in range(CORES):
                    if g == W_KV:
                        half = src.at[:, qcols + c * HD : qcols + (c + 1) * HD]
                    elif g == W_Q:
                        half = src.at[:, c * qcols // 2 : (c + 1) * qcols // 2]
                    else:
                        half = src.at[c * (tokens // 2) : (c + 1) * (tokens // 2), :]
                    n = half.shape[0]
                    part = pl.ds(pl.multiple_of(core * n, n), n)
                    copies.append((d, c, half, own[g].at[0, y, part], own_recv.at[g, 0, y]))
        for i, (d, c, half, dst, sem) in enumerate(copies):
            chip = z * PLANE + ((y + d) % NY) * CORES
            remote = functools.partial(
                pltpu.make_async_remote_copy,
                src_ref=half,
                dst_ref=dst,
                send_sem=plane_send.at[g, i],
                recv_sem=sem,
                device_id=device(chip + c, t),
            )
            local = functools.partial(pltpu.make_async_copy, half, dst, sem)
            yield d, c, remote, local

    def start_plane(g, src):
        for d, c, remote, local in plane_copies(g, src):
            if d == 0:
                pl.when(core == c)(lambda: local().start())
                pl.when(core != c)(lambda: remote().start())
            else:
                remote().start()

    def finish_plane(g, src):
        for d, c, remote, local in plane_copies(g, src):
            if d == 0:
                pl.when(core != c)(lambda: remote().wait_send())
            else:
                remote().wait_send()

    def take(g, q, j):
        unit = own[g].at[q, j]
        pltpu.make_async_copy(unit, unit, own_recv.at[g, q, j]).wait()
        pltpu.make_async_remote_copy(
            src_ref=unit,
            dst_ref=sib[g].at[q, j],
            send_sem=sib_send.at[g],
            recv_sem=sib_recv.at[g, q],
            device_id=device(sibling, t),
        ).start()

    def forward(g, q, j, to, q_there):
        pltpu.make_async_remote_copy(
            src_ref=own[g].at[q, j],
            dst_ref=own[g].at[q_there, j],
            send_sem=ring_send.at[g],
            recv_sem=own_recv.at[g, q_there, j],
            device_id=device(to, t),
        ).start()

    def when(condition, act):
        if isinstance(condition, bool):
            if condition:
                act()
        else:
            pl.when(condition)(act)

    def pass_unit(g, s, i):
        first = i < NY // 2
        j = (y + (i + i // 2 * (1 - 2 * (i % 2)) if NY == 4 else i)) % NY
        going_up = (s < H - 1) | ((s == H - 1) & first)
        going_down = (s < H - 1) | ((s == H - 1) & (i >= NY // 2))

        def nearest():
            take(g, 0, j)
            when(going_up, lambda: forward(g, 0, j, above, 1))
            when(going_down, lambda: forward(g, 0, j, below, NZ - 1))

        def between():
            take(g, s, j)
            when(going_up, lambda: forward(g, s, j, above, s + 1))
            take(g, NZ - s, j)
            when(going_down, lambda: forward(g, NZ - s, j, below, NZ - s - 1))

        when(s == 0, nearest)
        when((s > 0) & (s < H), between)
        when(s == H, lambda: take(g, H, j))

    def pass_on(g, s, lo=0, hi=NY):
        def body(i, carry):
            pass_unit(g, s, i)
            return carry

        if hi - lo == 1:
            pass_unit(g, s, lo)
        else:
            lax.fori_loop(lo, hi, body, 0)

    def for_slots(s, act):
        def body(i, carry):
            act(s + i * (NZ - 2 * s))
            return carry

        if isinstance(s, int):
            lax.fori_loop(0, 2 if 0 < s < H else 1, body, 0)
        else:
            lax.fori_loop(0, 2 - (s // H) - (1 - (s + H - 1) // H), body, 0)

    def wait_sibling(g, q):
        whole = sib[g].at[q]
        pltpu.make_async_copy(whole, whole, sib_recv.at[g, q]).wait()

    def finish_gather(g):
        sent = own[g].at[pl.ds(0, NZ - 1)]
        pltpu.make_async_copy(sent, sent, ring_send.at[g]).wait()
        pltpu.make_async_copy(sib[g], sib[g], sib_send.at[g]).wait()

    def source_z(q):
        return (z + NZ - q) % NZ

    start_plane(W_KV, w_in_ref)
    start_plane(W_Q, w_in_ref)
    pass_on(W_KV, 0, 0, 1)
    pass_on(W_Q, 0, 0, 1)

    for load in loads:
        load.wait()
    wide = hidden_ref[...].astype(jnp.float32)
    meansq = jnp.mean(wide * wide, axis=-1, keepdims=True)
    gain = gain_ref[...].astype(jnp.float32).reshape(1, D)
    normed_ref[t] = (wide * lax.rsqrt(meansq + 1e-5) * gain).astype(jnp.bfloat16)

    def norm_copy(d):
        return pltpu.make_async_remote_copy(
            src_ref=normed_ref.at[t],
            dst_ref=normed_ref.at[t],
            send_sem=norm_send.at[d - 1],
            recv_sem=norm_recv.at[t],
            device_id=device(ctx, (t + d) % NT),
        )

    for d in range(1, NT):
        norm_copy(d).start()

    pass_on(W_KV, 1, 0, 1)
    pass_on(W_KV, 0, 1)
    start_plane(W_OUT, w_out_ref)

    row = lax.broadcasted_iota(jnp.int32, (tokens, 1), 0)
    source = jnp.zeros_like(row)
    for a in range(tokens // SPAN):
        source = jnp.where(row // SPAN == a, span_ref[ctx * (tokens // SPAN) + a], source)
    orig = source * SPAN + row % SPAN
    start = jnp.zeros_like(orig)
    end = jnp.int32(0)
    for i in range(len_ref.shape[0]):
        end = end + len_ref[i]
        start = jnp.where(end <= orig, jnp.maximum(start, end), start)

    angle = (orig - start).astype(jnp.float32) * freq_ref[...]
    lane = lax.broadcasted_iota(jnp.int32, (tokens, HD), 1)
    cos_ref[...] = jnp.cos(angle)
    sine = jnp.sin(angle)
    sin_ref[...] = jnp.where(lane < HD // 2, -sine, sine)

    acc_kv[...] = jnp.zeros_like(acc_kv)
    acc_q[...] = jnp.zeros_like(acc_q)
    top_ref[...] = jnp.full_like(top_ref, MASKED)
    sum_ref[...] = jnp.zeros_like(sum_ref)
    o_ref[...] = jnp.zeros_like(o_ref)

    def project(g, acc, q):
        wait_sibling(g, q)
        cols = pl.ds(pl.multiple_of(source_z(q) * piece_k, piece_k), piece_k)
        left = normed_ref[:, :, cols].reshape(tokens, piece_k)
        for c, ref in ((core, own[g]), (1 - core, sib[g])):
            right = ref[q].reshape(piece_k, ref.shape[-1])
            acc[c] += jnp.dot(left, right, preferred_element_type=jnp.float32)

    project_kv = functools.partial(project, W_KV, acc_kv)
    project_q = functools.partial(project, W_Q, acc_q)

    scale = math.log2(math.e) / HD**0.5

    def rotate(x):
        return x * cos_ref[...] + pltpu.roll(x, HD // 2, 1) * sin_ref[...]

    for s in range(2, H + 1):
        pass_on(W_KV, s, 0, 1)
        pass_on(W_KV, s - 1, 1)
        pass_on(W_Q, s - 2, 1 if s == 2 else 0)
    for d in range(1, NT):
        other = (t + NT - d) % NT
        block = normed_ref.at[other]
        pltpu.make_async_copy(block, block, norm_recv.at[other]).wait()
    for s in range(H - 1):
        for_slots(s, project_kv)
    pass_on(W_KV, H, 1)
    for s in range(H - 1, H + 1):
        for_slots(s, project_kv)
    kv_stage[:, :HD] = rotate(acc_kv[0]).astype(jnp.bfloat16)
    kv_stage[:, HD:] = acc_kv[1].astype(jnp.bfloat16)
    start_plane(KV, kv_stage)

    pass_on(W_Q, H - 1)
    pass_on(W_OUT, 0)
    for s in range(H - 2):
        for_slots(s, project_q)
    pass_on(KV, 0, 0, 1)
    pass_on(W_Q, H)
    for s in range(H - 2, H + 1):
        for_slots(s, project_q)
    for h in range(HEADS_HERE):
        per = HEADS_HERE // 2
        x = acc_q[h // per, :, (h % per) * HD : (h % per + 1) * HD]
        q_ref[h * tokens : (h + 1) * tokens, :] = (rotate(x) * scale).astype(jnp.bfloat16)

    keys = J * tokens
    spans = keys // SPAN

    def attend_half(at, c, ref, q):
        lane = lax.broadcasted_iota(jnp.int32, (1, keys), 1)
        key_source = jnp.zeros_like(lane)
        for a in range(spans):
            held = span_ref[2 * (at * spans + a) + c]
            key_source = jnp.where(lane // SPAN == a, held, key_source)
        key_orig = key_source * SPAN + lane % SPAN
        allowed = (start <= key_orig) & (key_orig <= orig)
        cap = jnp.where(allowed, 3e38, MASKED)
        k = ref[q, :, :, :HD].reshape(keys, HD)
        v = ref[q, :, :, HD:].reshape(keys, HD)
        scores = lax.dot_general(q_ref[...], k, NT_DIMS, preferred_element_type=jnp.float32)
        weights = []
        for h in range(HEADS_HERE):
            rows_h = slice(h * tokens, (h + 1) * tokens)
            mine = jnp.minimum(scores[rows_h], cap)
            old = top_ref[rows_h, :]
            new = jnp.maximum(old, jnp.max(mine, axis=1, keepdims=True))
            fade = jnp.exp2(old - new)
            top_ref[rows_h, :] = new
            expo = [jnp.exp2(mine[:, i : i + HD] - new) for i in range(0, keys, HD)]
            sum_ref[rows_h, :] = sum_ref[rows_h, :] * fade + functools.reduce(jnp.add, expo)
            o_ref[rows_h, :] = o_ref[rows_h, :] * fade
            weights.append(jnp.concatenate([e.astype(jnp.bfloat16) for e in expo], axis=1))
        weights = jnp.concatenate(weights, axis=0)
        o_ref[...] += jnp.dot(weights, v, preferred_element_type=jnp.float32)

    def attend(q):
        attend_half(source_z(q), core, kv_own, q)
        wait_sibling(KV, q)
        attend_half(source_z(q), 1 - core, kv_sib, q)

    def attend_step(m, carry):
        pl.when(m <= H)(lambda: pass_on(KV, m, 0, 1))
        pl.when(m <= H + 1)(lambda: pass_on(KV, m - 1, 1))
        pl.when(m == min(2, H))(lambda: pass_on(W_OUT, 1))
        if H > 2:
            pl.when(m == H)(lambda: pass_on(W_OUT, 2))
        pl.when(m >= 2)(lambda: for_slots(m - 2, attend))
        return carry

    lax.fori_loop(1, H + 3, attend_step, 0)
    for h in range(HEADS_HERE):
        at = pl.ds(h * tokens, tokens)
        mixed_ref[:, h * HD : (h + 1) * HD] = (
            o_ref[at, :] / jnp.sum(sum_ref[at, :], axis=1, keepdims=True)
        ).astype(jnp.bfloat16)

    def rs_copy(q, d):
        u = (t + d) % NT
        return pltpu.make_async_remote_copy(
            src_ref=rs_send.at[q, u],
            dst_ref=rs_recv.at[q, d - 1],
            send_sem=rs_send_sem,
            recv_sem=rs_recv_sem.at[q],
            device_id=device(ctx, u),
        )

    def share(q):
        wait_sibling(W_OUT, q)
        for i, ref in enumerate((w_out_own, w_out_sib)):
            right = ref[q].reshape(half_c, ref.shape[-1])
            part = lax.dot_general(mixed_ref[...], right, NT_DIMS, preferred_element_type=jnp.float32)
            part = part.astype(jnp.bfloat16).reshape(NT, rows, half_c)
            rs_send[q, :, :, i * half_c : (i + 1) * half_c] = part
        for d in range(1, NT):
            rs_copy(q, d).start()

    def add_up(q):
        whole = rs_recv.at[q]
        pltpu.make_async_copy(whole, whole, rs_recv_sem.at[q]).wait()
        total = rs_send[q, t].astype(jnp.float32)
        for d in range(1, NT):
            total += rs_recv[q, d - 1].astype(jnp.float32)
        total = total.astype(jnp.bfloat16)
        for i, c in enumerate((core, 1 - core)):
            cols = pl.ds(pl.multiple_of((source_z(q) * 2 + c) * half_c, half_c), half_c)
            out_ref[:, cols] = total[:, i * half_c : (i + 1) * half_c]

    def share_step(s, carry):
        pl.when(s > min(2, H - 1))(lambda: pass_on(W_OUT, s))
        for_slots(s - 1, share)

        @pl.when(s > 2)
        def _():
            for_slots(s - 3, add_up)

        return carry

    lax.fori_loop(1, H + 1, share_step, 0)
    share(H)

    def add_step(s, carry):
        for_slots(s, add_up)
        return carry

    lax.fori_loop(max(H - 2, 0), H + 1, add_step, 0)

    finish_plane(W_KV, w_in_ref)
    finish_plane(W_Q, w_in_ref)
    finish_plane(W_OUT, w_out_ref)
    finish_plane(KV, kv_stage)
    for g in range(GATHERS):
        finish_gather(g)
    for d in range(1, NT):
        norm_copy(d).wait_send()
    pltpu.make_async_copy(rs_recv, rs_recv, rs_send_sem).wait()


def per_device(NC, NT, NY, hidden_rows, norm_gain, w_qkv, w_out, doc_lengths, span_order):
    J = NY * CORES // 2
    NZ = NC // (NY * CORES)
    rows, D = hidden_rows.shape
    tokens = rows * NT
    k_rows, in_cols = w_qkv.shape
    out_rows, c_cols = w_out.shape
    qcols = HEADS_HERE * HD
    freq = THETA ** (-(np.arange(HD // 2, dtype=np.float64) * 2.0 / HD))
    freq = jnp.asarray(np.tile(freq, 2)[None, :].astype(np.float32))
    bf16, f32 = jnp.bfloat16, jnp.float32
    vmem = pl.BlockSpec(memory_space=pltpu.VMEM)
    smem = pl.BlockSpec(memory_space=pltpu.SMEM)
    hbm = pl.BlockSpec(memory_space=pltpu.HBM)
    DMA = pltpu.SemaphoreType.DMA
    return pl.pallas_call(
        functools.partial(kernel, NZ, NY, NT),
        out_shape=jax.ShapeDtypeStruct((rows, D), bf16),
        in_specs=[smem, smem, hbm, hbm, hbm, hbm, hbm],
        out_specs=vmem,
        scratch_shapes=[
            pltpu.VMEM((rows, D), bf16),
            pltpu.VMEM((D,), bf16),
            pltpu.VMEM((1, HD), f32),
            pltpu.VMEM((tokens, HD), f32),
            pltpu.VMEM((tokens, HD), f32),
            pltpu.VMEM((NZ, NY, CORES * k_rows, HD), bf16),
            pltpu.VMEM((NZ, NY, CORES * k_rows, HD), bf16),
            pltpu.VMEM((NZ, NY, CORES * k_rows, qcols // 2), bf16),
            pltpu.VMEM((NZ, NY, CORES * k_rows, qcols // 2), bf16),
            pltpu.VMEM((NZ, NY, tokens, 2 * HD), bf16),
            pltpu.VMEM((NZ, NY, tokens, 2 * HD), bf16),
            pltpu.VMEM((NZ, J, c_cols, out_rows), bf16),
            pltpu.VMEM((NZ, J, c_cols, out_rows), bf16),
            pltpu.VMEM((NT, rows, D), bf16),
            pltpu.VMEM((CORES, tokens, HD), f32),
            pltpu.VMEM((CORES, tokens, qcols // 2), f32),
            pltpu.VMEM((HEADS_HERE * tokens, HD), bf16),
            pltpu.VMEM((tokens, 2 * HD), bf16),
            pltpu.VMEM((HEADS_HERE * tokens, HD), f32),
            pltpu.VMEM((HEADS_HERE * tokens, HD), f32),
            pltpu.VMEM((HEADS_HERE * tokens, HD), f32),
            pltpu.VMEM((tokens, qcols), bf16),
            pltpu.VMEM((NZ, NT, rows, 2 * J * c_cols), bf16),
            pltpu.VMEM((NZ, NT - 1, rows, 2 * J * c_cols), bf16),
            DMA((GATHERS, NZ, J)),
            DMA((GATHERS, NZ)),
            DMA((GATHERS, 2 * NY)),
            DMA((GATHERS,)),
            DMA((GATHERS,)),
            DMA((NT - 1,)),
            DMA((NT,)),
            DMA,
            DMA((NZ,)),
            DMA((3,)),
        ],
        compiler_params=pltpu.CompilerParams(
            collective_id=0, has_side_effects=True, vmem_limit_bytes=62 * 2**20
        ),
        cost_estimate=pl.CostEstimate(
            flops=2 * tokens * (D * in_cols + qcols * 2 * NC * tokens + out_rows * D),
            bytes_accessed=4 * rows * D,
            transcendentals=HEADS_HERE * tokens * tokens * NC,
        ),
    )(span_order, doc_lengths, hidden_rows, norm_gain, freq, w_qkv, w_out.T)


def build(mesh, NY):
    placed = (
        P(("context", "tensor"), None),
        P(),
        P("context", "tensor"),
        P("tensor", "context"),
        P(),
        P(),
    )
    return jax.shard_map(
        functools.partial(per_device, mesh.shape["context"], mesh.shape["tensor"], NY),
        mesh=mesh,
        in_specs=placed,
        out_specs=P(("context", "tensor"), None),
        check_vma=False,
    )


def solution(mesh):
    return build(mesh, Y_HI)
```

```python
import functools
import math

import jax
import jax.numpy as jnp
import numpy as np
from jax import lax
from jax.experimental import pallas as pl
from jax.experimental.pallas import tpu as pltpu
from jax.sharding import PartitionSpec as P

HD = 128
HEADS_HERE = 4
SPAN = 64
THETA = 500000.0
Y_HI = 4
CORES = 2
MASKED = -1e30
NT_DIMS = (((1,), (1,)), ((), ()))

W_KV, W_Q, KV, W_OUT = 0, 1, 2, 3
GATHERS = 4
Z_OUT = 0
Z_GATHERS = 1


def kernel(
    NZ,
    NY,
    NT,
    span_ref,
    len_ref,
    hidden_hbm,
    gain_hbm,
    freq_hbm,
    w_in_ref,
    w_out_ref,
    out_ref,
    hidden_ref,
    gain_ref,
    freq_ref,
    cos_ref,
    sin_ref,
    w_kv_own,
    w_kv_sib,
    w_q_own,
    w_q_sib,
    kv_own,
    kv_sib,
    w_out_own,
    w_out_sib,
    z_out,
    normed_ref,
    acc_kv,
    acc_q,
    q_ref,
    kv_stage,
    o_ref,
    top_ref,
    sum_ref,
    mixed_ref,
    rs_send,
    rs_recv,
    own_recv,
    sib_recv,
    plane_send,
    ring_send,
    sib_send,
    norm_send,
    norm_recv,
    rs_send_sem,
    rs_recv_sem,
    load_sem,
    z_recv,
    y_recv,
    z_sib_recv,
    z_send,
    y_send,
    far_send,
    z_sib_send,
):
    PLANE = NY * CORES
    J = PLANE // 2
    rows, D = hidden_ref.shape
    tokens = rows * NT
    qcols = HEADS_HERE * HD
    piece_k = D // NZ
    half_c = J * w_out_ref.shape[0]
    order = (0, 1, 3, 2) if NY == 4 else (0, 1)
    H = NZ // 2

    ctx = lax.axis_index("context")
    t = lax.axis_index("tensor")
    z = ctx // PLANE
    y = (ctx % PLANE) // CORES
    core = ctx % CORES
    my_class = y // (NY // 2)
    slot = (y % (NY // 2)) * CORES + core
    above = ((z + 1) % NZ) * PLANE + y * CORES + core
    below = ((z + NZ - 1) % NZ) * PLANE + y * CORES + core
    sibling = z * PLANE + y * CORES + (1 - core)

    def device(c, u):
        return {"context": c, "tensor": u}

    loads = [
        pltpu.make_async_copy(src, dst, load_sem.at[i])
        for i, (src, dst) in enumerate(
            ((hidden_hbm, hidden_ref), (gain_hbm, gain_ref), (freq_hbm, freq_ref))
        )
    ]
    for load in loads:
        load.start()

    own = (w_kv_own, w_q_own, kv_own, w_out_own)
    sib = (w_kv_sib, w_q_sib, kv_sib, w_out_sib)

    barrier = pltpu.get_barrier_semaphore()
    for d in range(1, PLANE):
        c = z * PLANE + (ctx % PLANE + d) % PLANE
        pl.semaphore_signal(barrier, inc=1, device_id=device(c, t))
    for c in (above, below):
        pl.semaphore_signal(barrier, inc=1, device_id=device(c, t))
    for d in range(1, NT):
        pl.semaphore_signal(barrier, inc=1, device_id=device(ctx, (t + d) % NT))

    pl.semaphore_wait(barrier, PLANE - 1 + 2 + NT - 1)

    def plane_copies(g, src):
        copies = []
        if g == W_OUT:
            for d in order:
                copies.append((d, my_class, src, own[g].at[0, slot], own_recv.at[g, 0, slot]))
        else:
            for d in order:
                for c in range(CORES):
                    if g == W_KV:
                        half = src.at[:, qcols + c * HD : qcols + (c + 1) * HD]
                    elif g == W_Q:
                        half = src.at[:, c * qcols // 2 : (c + 1) * qcols // 2]
                    else:
                        half = src.at[c * (tokens // 2) : (c + 1) * (tokens // 2), :]
                    n = half.shape[0]
                    part = pl.ds(pl.multiple_of(core * n, n), n)
                    copies.append((d, c, half, own[g].at[0, y, part], own_recv.at[g, 0, y]))
        for i, (d, c, half, dst, sem) in enumerate(copies):
            chip = z * PLANE + ((y + d) % NY) * CORES
            remote = functools.partial(
                pltpu.make_async_remote_copy,
                src_ref=half,
                dst_ref=dst,
                send_sem=plane_send.at[g, i],
                recv_sem=sem,
                device_id=device(chip + c, t),
            )
            local = functools.partial(pltpu.make_async_copy, half, dst, sem)
            yield d, c, remote, local

    def start_plane(g, src):
        for d, c, remote, local in plane_copies(g, src):
            if d == 0:
                pl.when(core == c)(lambda: local().start())
                pl.when(core != c)(lambda: remote().start())
            else:
                remote().start()

    def finish_plane(g, src):
        for d, c, remote, local in plane_copies(g, src):
            if d == 0:
                pl.when(core != c)(lambda: remote().wait_send())
            else:
                remote().wait_send()

    def take(g, q, j):
        unit = own[g].at[q, j]
        pltpu.make_async_copy(unit, unit, own_recv.at[g, q, j]).wait()
        pltpu.make_async_remote_copy(
            src_ref=unit,
            dst_ref=sib[g].at[q, j],
            send_sem=sib_send.at[g],
            recv_sem=sib_recv.at[g, q],
            device_id=device(sibling, t),
        ).start()

    def forward(g, q, j, to, q_there):
        pltpu.make_async_remote_copy(
            src_ref=own[g].at[q, j],
            dst_ref=own[g].at[q_there, j],
            send_sem=ring_send.at[g],
            recv_sem=own_recv.at[g, q_there, j],
            device_id=device(to, t),
        ).start()

    def when(condition, act):
        if isinstance(condition, bool):
            if condition:
                act()
        else:
            pl.when(condition)(act)

    def pass_unit(g, s, i):
        first = i < NY // 2
        j = (y + (i + i // 2 * (1 - 2 * (i % 2)) if NY == 4 else i)) % NY
        going_up = (s < H - 1) | ((s == H - 1) & first)
        going_down = (s < H - 1) | ((s == H - 1) & (i >= NY // 2))

        def nearest():
            take(g, 0, j)
            when(going_up, lambda: forward(g, 0, j, above, 1))
            when(going_down, lambda: forward(g, 0, j, below, NZ - 1))

        def between():
            take(g, s, j)
            when(going_up, lambda: forward(g, s, j, above, s + 1))
            take(g, NZ - s, j)
            when(going_down, lambda: forward(g, NZ - s, j, below, NZ - s - 1))

        when(s == 0, nearest)
        when((s > 0) & (s < H), between)
        when(s == H, lambda: take(g, H, j))

    def pass_on(g, s, lo=0, hi=NY):
        def body(i, carry):
            pass_unit(g, s, i)
            return carry

        if hi - lo == 1:
            pass_unit(g, s, lo)
        else:
            lax.fori_loop(lo, hi, body, 0)

    def for_slots(s, act):
        def body(i, carry):
            act(s + i * (NZ - 2 * s))
            return carry

        if isinstance(s, int):
            lax.fori_loop(0, 2 if 0 < s < H else 1, body, 0)
        else:
            lax.fori_loop(0, 2 - (s // H) - (1 - (s + H - 1) // H), body, 0)

    def wait_sibling(g, q):
        whole = sib[g].at[q]
        pltpu.make_async_copy(whole, whole, sib_recv.at[g, q]).wait()

    def finish_gather(g):
        sent = own[g].at[pl.ds(0, NZ - 1)]
        pltpu.make_async_copy(sent, sent, ring_send.at[g]).wait()
        pltpu.make_async_copy(sib[g], sib[g], sib_send.at[g]).wait()

    def source_z(q):
        return (z + NZ - q) % NZ

    held = (z_out,)
    near = (1, NY - 1) if NY > 2 else (1,)

    def z_local(g, src):
        return pltpu.make_async_copy(src, held[g].at[0, y, core], z_recv.at[g, 0])

    def z_copy(g, src_place, dst_place, send_sem, recv_sem, to):
        pltpu.make_async_remote_copy(
            src_ref=held[g].at[src_place],
            dst_ref=held[g].at[dst_place],
            send_sem=send_sem.at[g],
            recv_sem=recv_sem,
            device_id=device(to, t),
        ).start()

    def z_wait(g, place, sem):
        ref = held[g].at[place]
        pltpu.make_async_copy(ref, ref, sem).wait()

    def z_hand(g, q, row):
        z_copy(g, (q, row, core), (q, row, core), z_sib_send, z_sib_recv.at[g, q], sibling)

    def z_pass(g, s):
        going_up = (s < H - 1) | ((s == H - 1) & (core == 0))
        going_down = (s < H - 1) | ((s == H - 1) & (core == 1))

        def up(q):
            z_copy(g, (q, y, core), (q + 1, y, core), z_send, z_recv.at[g, q + 1], above)

        def down(q):
            there = (q + NZ - 1) % NZ
            z_copy(g, (q, y, core), (there, y, core), z_send, z_recv.at[g, there], below)

        def nearest():
            z_wait(g, (0, y, core), z_recv.at[g, 0])
            when(going_up, lambda: up(0))
            when(going_down, lambda: down(0))
            z_hand(g, 0, y)

        def between():
            z_wait(g, (s, y, core), z_recv.at[g, s])
            when(going_up, lambda: up(s))
            z_wait(g, (NZ - s, y, core), z_recv.at[g, NZ - s])
            when(going_down, lambda: down(NZ - s))
            z_hand(g, s, y)
            z_hand(g, NZ - s, y)

        def farthest():
            z_wait(g, (H, y, core), z_recv.at[g, H])
            z_hand(g, H, y)

        when(s == 0, nearest)
        when((s > 0) & (s < H), between)
        when(s == H, farthest)

    def chip_along_y(d):
        return z * PLANE + ((y + d) % NY) * CORES + core

    def y_push(g, q):
        for d in near:
            z_copy(g, (q, y, core), (q, y, core), y_send, y_recv.at[g, q, y], chip_along_y(d))

    def y_take(g, q):
        for d in near:
            row = (y + d) % NY
            z_wait(g, (q, row, core), y_recv.at[g, q, row])
            if NY > 2:

                @pl.when(q % 2 == (0 if d == 1 else 1))
                def _():
                    z_copy(g, (q, row, core), (q, row, core), far_send, y_recv.at[g, q, row], chip_along_y(NY - d))

            z_hand(g, q, row)

    def far_take(g, q):
        if NY > 2:
            row = (y + 2) % NY
            z_wait(g, (q, row, core), y_recv.at[g, q, row])
            z_hand(g, q, row)

    def z_wait_sibling(g, q):
        z_wait(g, (q, slice(None), 1 - core), z_sib_recv.at[g, q])

    def z_finish(g):
        for place, sem in (
            ((pl.ds(0, NZ - 1), 0, 0), z_send),
            ((slice(None), 0) if NY > 2 else (slice(None), 0, 0), y_send),
            ((slice(None), slice(None), 0), z_sib_send),
        ):
            z_wait(g, place, sem.at[g])
        if NY > 2:
            z_wait(g, (slice(None), 0, 0), far_send.at[g])

    def y_pushes(g, s):
        for_slots(s, functools.partial(y_push, g))

    def y_takes(g, s):
        for_slots(s, functools.partial(y_take, g))

    def far_takes(g, s):
        for_slots(s, functools.partial(far_take, g))

    w_out_first = w_out_ref.at[:, : qcols // 2]
    w_out_rest = w_out_ref.at[:, qcols // 2 : qcols]
    z_local(Z_OUT, w_out_rest).start()

    start_plane(W_KV, w_in_ref)
    start_plane(W_Q, w_in_ref)
    pass_on(W_KV, 0, 0, 1)
    pass_on(W_Q, 0, 0, 1)

    for load in loads:
        load.wait()
    wide = hidden_ref[...].astype(jnp.float32)
    meansq = jnp.mean(wide * wide, axis=-1, keepdims=True)
    gain = gain_ref[...].astype(jnp.float32).reshape(1, D)
    normed_ref[t] = (wide * lax.rsqrt(meansq + 1e-5) * gain).astype(jnp.bfloat16)

    def norm_copy(d):
        return pltpu.make_async_remote_copy(
            src_ref=normed_ref.at[t],
            dst_ref=normed_ref.at[t],
            send_sem=norm_send.at[d - 1],
            recv_sem=norm_recv.at[t],
            device_id=device(ctx, (t + d) % NT),
        )

    for d in range(1, NT):
        norm_copy(d).start()

    pass_on(W_KV, 1, 0, 1)
    pass_on(W_KV, 0, 1)
    z_pass(Z_OUT, 0)
    pass_on(W_Q, 1, 0, 1)

    row = lax.broadcasted_iota(jnp.int32, (tokens, 1), 0)
    source = jnp.zeros_like(row)
    for a in range(tokens // SPAN):
        source = jnp.where(row // SPAN == a, span_ref[ctx * (tokens // SPAN) + a], source)
    orig = source * SPAN + row % SPAN
    start = jnp.zeros_like(orig)
    end = jnp.int32(0)
    for i in range(len_ref.shape[0]):
        end = end + len_ref[i]
        start = jnp.where(end <= orig, jnp.maximum(start, end), start)

    angle = (orig - start).astype(jnp.float32) * freq_ref[...]
    lane = lax.broadcasted_iota(jnp.int32, (tokens, HD), 1)
    cos_ref[...] = jnp.cos(angle)
    sine = jnp.sin(angle)
    sin_ref[...] = jnp.where(lane < HD // 2, -sine, sine)

    acc_kv[...] = jnp.zeros_like(acc_kv)
    acc_q[...] = jnp.zeros_like(acc_q)
    top_ref[...] = jnp.full_like(top_ref, MASKED)
    sum_ref[...] = jnp.zeros_like(sum_ref)
    o_ref[...] = jnp.zeros_like(o_ref)

    def project(g, acc, q):
        wait_sibling(g, q)
        cols = pl.ds(pl.multiple_of(source_z(q) * piece_k, piece_k), piece_k)
        left = normed_ref[:, :, cols].reshape(tokens, piece_k)
        for c, ref in ((core, own[g]), (1 - core, sib[g])):
            right = ref[q].reshape(piece_k, ref.shape[-1])
            acc[c] += jnp.dot(left, right, preferred_element_type=jnp.float32)

    project_kv = functools.partial(project, W_KV, acc_kv)
    project_q = functools.partial(project, W_Q, acc_q)

    scale = math.log2(math.e) / HD**0.5

    def rotate(x):
        return x * cos_ref[...] + pltpu.roll(x, HD // 2, 1) * sin_ref[...]

    for s in range(2, H + 1):
        pass_on(W_KV, s, 0, 1)
        pass_on(W_KV, s - 1, 1)
        pass_on(W_Q, s, 0, 1)
        pass_on(W_Q, s - 2, 1)
        if s == 2:
            start_plane(W_OUT, w_out_first)
        z_pass(Z_OUT, s - 1)
        if s < 4:
            y_pushes(Z_OUT, s - 2)
    y_takes(Z_OUT, 0)
    pass_on(W_OUT, 0)
    for d in range(1, NT):
        other = (t + NT - d) % NT
        block = normed_ref.at[other]
        pltpu.make_async_copy(block, block, norm_recv.at[other]).wait()
    for s in range(H - 1):
        for_slots(s, project_kv)
    pass_on(W_KV, H, 1)
    for s in range(H - 1, H + 1):
        for_slots(s, project_kv)
    kv_stage[:, :HD] = rotate(acc_kv[0]).astype(jnp.bfloat16)
    kv_stage[:, HD:] = acc_kv[1].astype(jnp.bfloat16)
    start_plane(KV, kv_stage)

    pass_on(W_Q, H - 1, 1)
    z_pass(Z_OUT, H)
    for s in range(H - 2):
        for_slots(s, project_q)
    pass_on(KV, 0)
    y_pushes(Z_OUT, 2)
    pass_on(KV, 1, 0, 1)
    pass_on(W_Q, H, 1)
    far_takes(Z_OUT, 0)
    y_takes(Z_OUT, 1)
    for s in range(H - 2, H + 1):
        for_slots(s, project_q)
    for h in range(HEADS_HERE):
        per = HEADS_HERE // 2
        x = acc_q[h // per, :, (h % per) * HD : (h % per + 1) * HD]
        q_ref[h * tokens : (h + 1) * tokens, :] = (rotate(x) * scale).astype(jnp.bfloat16)

    keys = J * tokens
    spans = keys // SPAN

    def attend_half(at, c, ref, q):
        lane = lax.broadcasted_iota(jnp.int32, (1, keys), 1)
        key_source = jnp.zeros_like(lane)
        for a in range(spans):
            held = span_ref[2 * (at * spans + a) + c]
            key_source = jnp.where(lane // SPAN == a, held, key_source)
        key_orig = key_source * SPAN + lane % SPAN
        allowed = (start <= key_orig) & (key_orig <= orig)
        cap = jnp.where(allowed, 3e38, MASKED)
        k = ref[q, :, :, :HD].reshape(keys, HD)
        v = ref[q, :, :, HD:].reshape(keys, HD)
        scores = lax.dot_general(q_ref[...], k, NT_DIMS, preferred_element_type=jnp.float32)
        weights = []
        for h in range(HEADS_HERE):
            rows_h = slice(h * tokens, (h + 1) * tokens)
            mine = jnp.minimum(scores[rows_h], cap)
            old = top_ref[rows_h, :]
            new = jnp.maximum(old, jnp.max(mine, axis=1, keepdims=True))
            fade = jnp.exp2(old - new)
            top_ref[rows_h, :] = new
            expo = [jnp.exp2(mine[:, i : i + HD] - new) for i in range(0, keys, HD)]
            sum_ref[rows_h, :] = sum_ref[rows_h, :] * fade + functools.reduce(jnp.add, expo)
            o_ref[rows_h, :] = o_ref[rows_h, :] * fade
            weights.append(jnp.concatenate([e.astype(jnp.bfloat16) for e in expo], axis=1))
        weights = jnp.concatenate(weights, axis=0)
        o_ref[...] += jnp.dot(weights, v, preferred_element_type=jnp.float32)

    def attend(q):
        attend_half(source_z(q), core, kv_own, q)
        wait_sibling(KV, q)
        attend_half(source_z(q), 1 - core, kv_sib, q)

    def attend_step(m, carry):
        pl.when(m <= H)(lambda: pass_on(KV, m, 0, 1))
        pl.when(m <= H + 1)(lambda: pass_on(KV, m - 1, 1))
        pl.when(m == min(2, H))(lambda: pass_on(W_OUT, 1))
        if H == 4:
            pl.when(m == H - 1)(lambda: pass_on(W_OUT, 2))
            pl.when(m == H + 1)(lambda: pass_on(W_OUT, 3))
        pl.when(m < H)(lambda: y_pushes(Z_OUT, m + 1))
        pl.when((m >= 3) & (m <= H + 1))(lambda: y_takes(Z_OUT, m - 1))
        pl.when(m >= 3)(lambda: far_takes(Z_OUT, m - 2))
        for_slots(m - 2, attend)
        return carry

    lax.fori_loop(2, H + 3, attend_step, 0)
    for h in range(HEADS_HERE):
        at = pl.ds(h * tokens, tokens)
        mixed_ref[:, h * HD : (h + 1) * HD] = (
            o_ref[at, :] / jnp.sum(sum_ref[at, :], axis=1, keepdims=True)
        ).astype(jnp.bfloat16)

    def rs_copy(q, d):
        u = (t + d) % NT
        return pltpu.make_async_remote_copy(
            src_ref=rs_send.at[q, u],
            dst_ref=rs_recv.at[q, d - 1],
            send_sem=rs_send_sem,
            recv_sem=rs_recv_sem.at[q],
            device_id=device(ctx, u),
        )

    def share(q):
        wait_sibling(W_OUT, q)
        z_wait_sibling(Z_OUT, q)
        for i, (c, ref) in enumerate(((core, w_out_own), (1 - core, w_out_sib))):
            n = qcols // 2
            right = ref[q].reshape(half_c, n)
            part = lax.dot_general(mixed_ref[:, :n], right, NT_DIMS, preferred_element_type=jnp.float32)
            right = z_out[q, pl.ds(c * (NY // 2), NY // 2)].reshape(half_c, n)
            part += lax.dot_general(mixed_ref[:, n:], right, NT_DIMS, preferred_element_type=jnp.float32)
            part = part.astype(jnp.bfloat16).reshape(NT, rows, half_c)
            rs_send[q, :, :, i * half_c : (i + 1) * half_c] = part
        for d in range(1, NT):
            rs_copy(q, d).start()

    def add_up(q):
        whole = rs_recv.at[q]
        pltpu.make_async_copy(whole, whole, rs_recv_sem.at[q]).wait()
        total = rs_send[q, t].astype(jnp.float32)
        for d in range(1, NT):
            total += rs_recv[q, d - 1].astype(jnp.float32)
        total = total.astype(jnp.bfloat16)
        for i, c in enumerate((core, 1 - core)):
            cols = pl.ds(pl.multiple_of((source_z(q) * 2 + c) * half_c, half_c), half_c)
            out_ref[:, cols] = total[:, i * half_c : (i + 1) * half_c]

    def share_step(s, carry):
        pl.when(s > (3 if H == 4 else 1))(lambda: pass_on(W_OUT, s))
        for_slots(s - 1, share)

        @pl.when(s > 2)
        def _():
            for_slots(s - 3, add_up)

        return carry

    lax.fori_loop(1, H + 1, share_step, 0)
    share(H)

    def add_step(s, carry):
        for_slots(s, add_up)
        return carry

    lax.fori_loop(max(H - 2, 0), H + 1, add_step, 0)

    finish_plane(W_KV, w_in_ref)
    finish_plane(W_Q, w_in_ref)
    finish_plane(W_OUT, w_out_first)
    finish_plane(KV, kv_stage)
    for g in range(GATHERS):
        finish_gather(g)
    for g in range(Z_GATHERS):
        z_finish(g)
    for d in range(1, NT):
        norm_copy(d).wait_send()
    pltpu.make_async_copy(rs_recv, rs_recv, rs_send_sem).wait()


def per_device(NC, NT, NY, hidden_rows, norm_gain, w_qkv, w_out, doc_lengths, span_order):
    J = NY * CORES // 2
    NZ = NC // (NY * CORES)
    rows, D = hidden_rows.shape
    tokens = rows * NT
    k_rows, in_cols = w_qkv.shape
    out_rows, c_cols = w_out.shape
    qcols = HEADS_HERE * HD
    freq = THETA ** (-(np.arange(HD // 2, dtype=np.float64) * 2.0 / HD))
    freq = jnp.asarray(np.tile(freq, 2)[None, :].astype(np.float32))
    bf16, f32 = jnp.bfloat16, jnp.float32
    vmem = pl.BlockSpec(memory_space=pltpu.VMEM)
    smem = pl.BlockSpec(memory_space=pltpu.SMEM)
    hbm = pl.BlockSpec(memory_space=pltpu.HBM)
    DMA = pltpu.SemaphoreType.DMA
    return pl.pallas_call(
        functools.partial(kernel, NZ, NY, NT),
        out_shape=jax.ShapeDtypeStruct((rows, D), bf16),
        in_specs=[smem, smem, hbm, hbm, hbm, hbm, hbm],
        out_specs=vmem,
        scratch_shapes=[
            pltpu.VMEM((rows, D), bf16),
            pltpu.VMEM((D,), bf16),
            pltpu.VMEM((1, HD), f32),
            pltpu.VMEM((tokens, HD), f32),
            pltpu.VMEM((tokens, HD), f32),
            pltpu.VMEM((NZ, NY, CORES * k_rows, HD), bf16),
            pltpu.VMEM((NZ, NY, CORES * k_rows, HD), bf16),
            pltpu.VMEM((NZ, NY, CORES * k_rows, qcols // 2), bf16),
            pltpu.VMEM((NZ, NY, CORES * k_rows, qcols // 2), bf16),
            pltpu.VMEM((NZ, NY, tokens, 2 * HD), bf16),
            pltpu.VMEM((NZ, NY, tokens, 2 * HD), bf16),
            pltpu.VMEM((NZ, J, c_cols, out_rows // 2), bf16),
            pltpu.VMEM((NZ, J, c_cols, out_rows // 2), bf16),
            pltpu.VMEM((NZ, NY, CORES, c_cols, out_rows // 2), bf16),
            pltpu.VMEM((NT, rows, D), bf16),
            pltpu.VMEM((CORES, tokens, HD), f32),
            pltpu.VMEM((CORES, tokens, qcols // 2), f32),
            pltpu.VMEM((HEADS_HERE * tokens, HD), bf16),
            pltpu.VMEM((tokens, 2 * HD), bf16),
            pltpu.VMEM((HEADS_HERE * tokens, HD), f32),
            pltpu.VMEM((HEADS_HERE * tokens, HD), f32),
            pltpu.VMEM((HEADS_HERE * tokens, HD), f32),
            pltpu.VMEM((tokens, qcols), bf16),
            pltpu.VMEM((NZ, NT, rows, 2 * J * c_cols), bf16),
            pltpu.VMEM((NZ, NT - 1, rows, 2 * J * c_cols), bf16),
            DMA((GATHERS, NZ, J)),
            DMA((GATHERS, NZ)),
            DMA((GATHERS, 2 * NY)),
            DMA((GATHERS,)),
            DMA((GATHERS,)),
            DMA((NT - 1,)),
            DMA((NT,)),
            DMA,
            DMA((NZ,)),
            DMA((3,)),
            DMA((Z_GATHERS, NZ)),
            DMA((Z_GATHERS, NZ, NY)),
            DMA((Z_GATHERS, NZ)),
            DMA((Z_GATHERS,)),
            DMA((Z_GATHERS,)),
            DMA((Z_GATHERS,)),
            DMA((Z_GATHERS,)),
        ],
        compiler_params=pltpu.CompilerParams(
            collective_id=0, has_side_effects=True, vmem_limit_bytes=62 * 2**20
        ),
        cost_estimate=pl.CostEstimate(
            flops=2 * tokens * (D * in_cols + qcols * 2 * NC * tokens + out_rows * D),
            bytes_accessed=4 * rows * D,
            transcendentals=HEADS_HERE * tokens * tokens * NC,
        ),
    )(span_order, doc_lengths, hidden_rows, norm_gain, freq, w_qkv, w_out.T)


def build(mesh, NY):
    placed = (
        P(("context", "tensor"), None),
        P(),
        P("context", "tensor"),
        P("tensor", "context"),
        P(),
        P(),
    )
    return jax.shard_map(
        functools.partial(per_device, mesh.shape["context"], mesh.shape["tensor"], NY),
        mesh=mesh,
        in_specs=placed,
        out_specs=P(("context", "tensor"), None),
        check_vma=False,
    )


def solution(mesh):
    return build(mesh, Y_HI)
```

```python
import functools
import math

import jax
import jax.numpy as jnp
import numpy as np
from jax import lax
from jax.experimental import pallas as pl
from jax.experimental.pallas import tpu as pltpu
from jax.sharding import PartitionSpec as P

HD = 128
HEADS_HERE = 4
SPAN = 64
THETA = 500000.0
Y_HI = 4
CORES = 2
MASKED = -1e30
NT_DIMS = (((1,), (1,)), ((), ()))

W_KV, W_Q, KV, W_OUT = 0, 1, 2, 3
GATHERS = 4
Z_OUT = 0
Z_GATHERS = 1


def kernel(
    NZ,
    NY,
    NT,
    span_ref,
    len_ref,
    hidden_hbm,
    gain_hbm,
    freq_hbm,
    w_in_ref,
    w_out_ref,
    out_ref,
    hidden_ref,
    gain_ref,
    freq_ref,
    cos_ref,
    sin_ref,
    w_kv_own,
    w_kv_sib,
    w_q_own,
    w_q_sib,
    kv_own,
    kv_sib,
    w_out_own,
    w_out_sib,
    z_out,
    normed_ref,
    acc_kv,
    acc_q,
    q_ref,
    kv_stage,
    o_ref,
    top_ref,
    sum_ref,
    mixed_ref,
    rs_send,
    rs_recv,
    own_recv,
    sib_recv,
    plane_send,
    ring_send,
    sib_send,
    norm_send,
    norm_recv,
    rs_send_sem,
    rs_recv_sem,
    load_sem,
    z_recv,
    y_recv,
    z_sib_recv,
    z_send,
    y_send,
    far_send,
    z_sib_send,
):
    PLANE = NY * CORES
    J = PLANE // 2
    rows, D = hidden_ref.shape
    tokens = rows * NT
    qcols = HEADS_HERE * HD
    piece_k = D // NZ
    half_c = J * w_out_ref.shape[0]
    order = (0, 1, 3, 2) if NY == 4 else (0, 1)
    H = NZ // 2

    ctx = lax.axis_index("context")
    t = lax.axis_index("tensor")
    z = ctx // PLANE
    y = (ctx % PLANE) // CORES
    core = ctx % CORES
    my_class = y // (NY // 2)
    slot = (y % (NY // 2)) * CORES + core
    above = ((z + 1) % NZ) * PLANE + y * CORES + core
    below = ((z + NZ - 1) % NZ) * PLANE + y * CORES + core
    sibling = z * PLANE + y * CORES + (1 - core)

    def device(c, u):
        return {"context": c, "tensor": u}

    loads = [
        pltpu.make_async_copy(src, dst, load_sem.at[i])
        for i, (src, dst) in enumerate(
            ((hidden_hbm, hidden_ref), (gain_hbm, gain_ref), (freq_hbm, freq_ref))
        )
    ]
    for load in loads:
        load.start()

    own = (w_kv_own, w_q_own, kv_own, w_out_own)
    sib = (w_kv_sib, w_q_sib, kv_sib, w_out_sib)

    barrier = pltpu.get_barrier_semaphore()
    for d in range(1, PLANE):
        c = z * PLANE + (ctx % PLANE + d) % PLANE
        pl.semaphore_signal(barrier, inc=1, device_id=device(c, t))
    for c in (above, below):
        pl.semaphore_signal(barrier, inc=1, device_id=device(c, t))
    for d in range(1, NT):
        pl.semaphore_signal(barrier, inc=1, device_id=device(ctx, (t + d) % NT))

    pl.semaphore_wait(barrier, PLANE - 1 + 2 + NT - 1)

    def plane_copies(g, src):
        copies = []
        if g == W_OUT:
            for d in order:
                copies.append((d, my_class, src, own[g].at[0, slot], own_recv.at[g, 0, slot]))
        else:
            for d in order:
                for c in range(CORES):
                    if g == W_KV:
                        half = src.at[:, qcols + c * HD : qcols + (c + 1) * HD]
                    elif g == W_Q:
                        half = src.at[:, c * qcols // 2 : (c + 1) * qcols // 2]
                    else:
                        half = src.at[c * (tokens // 2) : (c + 1) * (tokens // 2), :]
                    n = half.shape[0]
                    part = pl.ds(pl.multiple_of(core * n, n), n)
                    copies.append((d, c, half, own[g].at[0, y, part], own_recv.at[g, 0, y]))
        for i, (d, c, half, dst, sem) in enumerate(copies):
            chip = z * PLANE + ((y + d) % NY) * CORES
            remote = functools.partial(
                pltpu.make_async_remote_copy,
                src_ref=half,
                dst_ref=dst,
                send_sem=plane_send.at[g, i],
                recv_sem=sem,
                device_id=device(chip + c, t),
            )
            local = functools.partial(pltpu.make_async_copy, half, dst, sem)
            yield d, c, remote, local

    def start_plane(g, src):
        for d, c, remote, local in plane_copies(g, src):
            if d == 0:
                pl.when(core == c)(lambda: local().start())
                pl.when(core != c)(lambda: remote().start())
            else:
                remote().start()

    def finish_plane(g, src):
        for d, c, remote, local in plane_copies(g, src):
            if d == 0:
                pl.when(core != c)(lambda: remote().wait_send())
            else:
                remote().wait_send()

    def take(g, q, j):
        unit = own[g].at[q, j]
        pltpu.make_async_copy(unit, unit, own_recv.at[g, q, j]).wait()
        pltpu.make_async_remote_copy(
            src_ref=unit,
            dst_ref=sib[g].at[q, j],
            send_sem=sib_send.at[g],
            recv_sem=sib_recv.at[g, q],
            device_id=device(sibling, t),
        ).start()

    def forward(g, q, j, to, q_there):
        pltpu.make_async_remote_copy(
            src_ref=own[g].at[q, j],
            dst_ref=own[g].at[q_there, j],
            send_sem=ring_send.at[g],
            recv_sem=own_recv.at[g, q_there, j],
            device_id=device(to, t),
        ).start()

    def when(condition, act):
        if isinstance(condition, bool):
            if condition:
                act()
        else:
            pl.when(condition)(act)

    def pass_unit(g, s, i):
        first = i < NY // 2
        j = (y + (i + i // 2 * (1 - 2 * (i % 2)) if NY == 4 else i)) % NY
        going_up = (s < H - 1) | ((s == H - 1) & first)
        going_down = (s < H - 1) | ((s == H - 1) & (i >= NY // 2))

        def nearest():
            take(g, 0, j)
            when(going_up, lambda: forward(g, 0, j, above, 1))
            when(going_down, lambda: forward(g, 0, j, below, NZ - 1))

        def between():
            take(g, s, j)
            when(going_up, lambda: forward(g, s, j, above, s + 1))
            take(g, NZ - s, j)
            when(going_down, lambda: forward(g, NZ - s, j, below, NZ - s - 1))

        when(s == 0, nearest)
        when((s > 0) & (s < H), between)
        when(s == H, lambda: take(g, H, j))

    def pass_on(g, s, lo=0, hi=NY):
        def body(i, carry):
            pass_unit(g, s, i)
            return carry

        if hi - lo == 1:
            pass_unit(g, s, lo)
        else:
            lax.fori_loop(lo, hi, body, 0)

    def for_slots(s, act):
        def body(i, carry):
            act(s + i * (NZ - 2 * s))
            return carry

        if isinstance(s, int):
            lax.fori_loop(0, 2 if 0 < s < H else 1, body, 0)
        else:
            lax.fori_loop(0, 2 - (s // H) - (1 - (s + H - 1) // H), body, 0)

    def wait_sibling(g, q):
        whole = sib[g].at[q]
        pltpu.make_async_copy(whole, whole, sib_recv.at[g, q]).wait()

    def finish_gather(g):
        sent = own[g].at[pl.ds(0, NZ - 1)]
        pltpu.make_async_copy(sent, sent, ring_send.at[g]).wait()
        pltpu.make_async_copy(sib[g], sib[g], sib_send.at[g]).wait()

    def source_z(q):
        return (z + NZ - q) % NZ

    held = (z_out,)
    near = (1, NY - 1) if NY > 2 else (1,)

    def z_local(g, src):
        return pltpu.make_async_copy(src, held[g].at[0, y, core], z_recv.at[g, 0])

    def z_copy(g, src_place, dst_place, send_sem, recv_sem, to):
        pltpu.make_async_remote_copy(
            src_ref=held[g].at[src_place],
            dst_ref=held[g].at[dst_place],
            send_sem=send_sem.at[g],
            recv_sem=recv_sem,
            device_id=device(to, t),
        ).start()

    def z_wait(g, place, sem):
        ref = held[g].at[place]
        pltpu.make_async_copy(ref, ref, sem).wait()

    def z_hand(g, q, row):
        z_copy(g, (q, row, core), (q, row, core), z_sib_send, z_sib_recv.at[g, q], sibling)

    def z_pass(g, s):
        going_up = (s < H - 1) | ((s == H - 1) & (core == 0))
        going_down = (s < H - 1) | ((s == H - 1) & (core == 1))

        def up(q):
            z_copy(g, (q, y, core), (q + 1, y, core), z_send, z_recv.at[g, q + 1], above)

        def down(q):
            there = (q + NZ - 1) % NZ
            z_copy(g, (q, y, core), (there, y, core), z_send, z_recv.at[g, there], below)

        def nearest():
            z_wait(g, (0, y, core), z_recv.at[g, 0])
            when(going_up, lambda: up(0))
            when(going_down, lambda: down(0))
            z_hand(g, 0, y)

        def between():
            z_wait(g, (s, y, core), z_recv.at[g, s])
            when(going_up, lambda: up(s))
            z_wait(g, (NZ - s, y, core), z_recv.at[g, NZ - s])
            when(going_down, lambda: down(NZ - s))
            z_hand(g, s, y)
            z_hand(g, NZ - s, y)

        def farthest():
            z_wait(g, (H, y, core), z_recv.at[g, H])
            z_hand(g, H, y)

        when(s == 0, nearest)
        when((s > 0) & (s < H), between)
        when(s == H, farthest)

    def chip_along_y(d):
        return z * PLANE + ((y + d) % NY) * CORES + core

    def y_push(g, q):
        for d in near:
            z_copy(g, (q, y, core), (q, y, core), y_send, y_recv.at[g, q, y], chip_along_y(d))

    def y_take(g, q):
        for d in near:
            row = (y + d) % NY
            z_wait(g, (q, row, core), y_recv.at[g, q, row])
            if NY > 2:

                @pl.when(q % 2 == (0 if d == 1 else 1))
                def _():
                    z_copy(g, (q, row, core), (q, row, core), far_send, y_recv.at[g, q, row], chip_along_y(NY - d))

            z_hand(g, q, row)

    def far_take(g, q):
        if NY > 2:
            row = (y + 2) % NY
            z_wait(g, (q, row, core), y_recv.at[g, q, row])
            z_hand(g, q, row)

    def z_wait_sibling(g, q):
        z_wait(g, (q, slice(None), 1 - core), z_sib_recv.at[g, q])

    def z_finish(g):
        for place, sem in (
            ((pl.ds(0, NZ - 1), 0, 0), z_send),
            ((slice(None), 0) if NY > 2 else (slice(None), 0, 0), y_send),
            ((slice(None), slice(None), 0), z_sib_send),
        ):
            z_wait(g, place, sem.at[g])
        if NY > 2:
            z_wait(g, (slice(None), 0, 0), far_send.at[g])

    def y_pushes(g, s):
        for_slots(s, functools.partial(y_push, g))

    def y_takes(g, s):
        for_slots(s, functools.partial(y_take, g))

    def far_takes(g, s):
        for_slots(s, functools.partial(far_take, g))

    w_out_first = w_out_ref.at[:, : qcols // 2]
    w_out_rest = w_out_ref.at[:, qcols // 2 : qcols]
    z_local(Z_OUT, w_out_rest).start()

    start_plane(W_KV, w_in_ref)
    start_plane(W_Q, w_in_ref)
    pass_on(W_KV, 0, 0, 1)
    pass_on(W_Q, 0, 0, 1)

    for load in loads:
        load.wait()
    wide = hidden_ref[...].astype(jnp.float32)
    meansq = jnp.mean(wide * wide, axis=-1, keepdims=True)
    gain = gain_ref[...].astype(jnp.float32).reshape(1, D)
    normed_ref[t] = (wide * lax.rsqrt(meansq + 1e-5) * gain).astype(jnp.bfloat16)

    def norm_copy(d):
        return pltpu.make_async_remote_copy(
            src_ref=normed_ref.at[t],
            dst_ref=normed_ref.at[t],
            send_sem=norm_send.at[d - 1],
            recv_sem=norm_recv.at[t],
            device_id=device(ctx, (t + d) % NT),
        )

    for d in range(1, NT):
        norm_copy(d).start()

    pass_on(W_KV, 1, 0, 1)
    pass_on(W_KV, 0, 1)
    z_pass(Z_OUT, 0)
    pass_on(W_Q, 1, 0, 1)

    row = lax.broadcasted_iota(jnp.int32, (tokens, 1), 0)
    source = jnp.zeros_like(row)
    for a in range(tokens // SPAN):
        source = jnp.where(row // SPAN == a, span_ref[ctx * (tokens // SPAN) + a], source)
    orig = source * SPAN + row % SPAN
    start = jnp.zeros_like(orig)
    end = jnp.int32(0)
    for i in range(len_ref.shape[0]):
        end = end + len_ref[i]
        start = jnp.where(end <= orig, jnp.maximum(start, end), start)

    angle = (orig - start).astype(jnp.float32) * freq_ref[...]
    lane = lax.broadcasted_iota(jnp.int32, (tokens, HD), 1)
    cos_ref[...] = jnp.cos(angle)
    sine = jnp.sin(angle)
    sin_ref[...] = jnp.where(lane < HD // 2, -sine, sine)

    acc_kv[...] = jnp.zeros_like(acc_kv)
    acc_q[...] = jnp.zeros_like(acc_q)
    top_ref[...] = jnp.full_like(top_ref, MASKED)
    sum_ref[...] = jnp.zeros_like(sum_ref)
    o_ref[...] = jnp.zeros_like(o_ref)

    def project(g, acc, q):
        wait_sibling(g, q)
        cols = pl.ds(pl.multiple_of(source_z(q) * piece_k, piece_k), piece_k)
        left = normed_ref[:, :, cols].reshape(tokens, piece_k)
        for c, ref in ((core, own[g]), (1 - core, sib[g])):
            right = ref[q].reshape(piece_k, ref.shape[-1])
            acc[c] += jnp.dot(left, right, preferred_element_type=jnp.float32)

    project_kv = functools.partial(project, W_KV, acc_kv)
    project_q = functools.partial(project, W_Q, acc_q)

    scale = math.log2(math.e) / HD**0.5

    def rotate(x):
        return x * cos_ref[...] + pltpu.roll(x, HD // 2, 1) * sin_ref[...]

    for s in range(2, H + 1):
        pass_on(W_KV, s, 0, 1)
        pass_on(W_KV, s - 1, 1)
        pass_on(W_Q, s, 0, 1)
        pass_on(W_Q, s - 2, 1)
        if s == 2:
            start_plane(W_OUT, w_out_first)
        z_pass(Z_OUT, s - 1)
        if s < 4:
            y_pushes(Z_OUT, s - 2)
    y_takes(Z_OUT, 0)
    pass_on(W_OUT, 0)
    for d in range(1, NT):
        other = (t + NT - d) % NT
        block = normed_ref.at[other]
        pltpu.make_async_copy(block, block, norm_recv.at[other]).wait()
    for s in range(H - 1):
        for_slots(s, project_kv)
    pass_on(W_KV, H, 1)
    for s in range(H - 1, H + 1):
        for_slots(s, project_kv)
    kv_stage[:, :HD] = rotate(acc_kv[0]).astype(jnp.bfloat16)
    kv_stage[:, HD:] = acc_kv[1].astype(jnp.bfloat16)
    start_plane(KV, kv_stage)

    pass_on(W_Q, H - 1, 1)
    z_pass(Z_OUT, H)
    for s in range(H - 2):
        for_slots(s, project_q)
    pass_on(KV, 0)
    y_pushes(Z_OUT, 2)
    pass_on(KV, 1, 0, 1)
    pass_on(W_Q, H, 1)
    far_takes(Z_OUT, 0)
    y_takes(Z_OUT, 1)
    for s in range(H - 2, H + 1):
        for_slots(s, project_q)
    for h in range(HEADS_HERE):
        per = HEADS_HERE // 2
        x = acc_q[h // per, :, (h % per) * HD : (h % per + 1) * HD]
        q_ref[h * tokens : (h + 1) * tokens, :] = (rotate(x) * scale).astype(jnp.bfloat16)

    keys = J * tokens
    spans = keys // SPAN

    def attend_half(at, c, ref, q):
        lane = lax.broadcasted_iota(jnp.int32, (1, keys), 1)
        key_source = jnp.zeros_like(lane)
        for a in range(spans):
            held = span_ref[2 * (at * spans + a) + c]
            key_source = jnp.where(lane // SPAN == a, held, key_source)
        key_orig = key_source * SPAN + lane % SPAN
        allowed = (start <= key_orig) & (key_orig <= orig)
        cap = jnp.where(allowed, 3e38, MASKED)
        k = ref[q, :, :, :HD].reshape(keys, HD)
        v = ref[q, :, :, HD:].reshape(keys, HD)
        scores = lax.dot_general(q_ref[...], k, NT_DIMS, preferred_element_type=jnp.float32)
        weights = []
        for h in range(HEADS_HERE):
            rows_h = slice(h * tokens, (h + 1) * tokens)
            mine = jnp.minimum(scores[rows_h], cap)
            old = top_ref[rows_h, :]
            new = jnp.maximum(old, jnp.max(mine, axis=1, keepdims=True))
            fade = jnp.exp2(old - new)
            top_ref[rows_h, :] = new
            expo = [jnp.exp2(mine[:, i : i + HD] - new) for i in range(0, keys, HD)]
            sum_ref[rows_h, :] = sum_ref[rows_h, :] * fade + functools.reduce(jnp.add, expo)
            o_ref[rows_h, :] = o_ref[rows_h, :] * fade
            weights.append(jnp.concatenate([e.astype(jnp.bfloat16) for e in expo], axis=1))
        weights = jnp.concatenate(weights, axis=0)
        o_ref[...] += jnp.dot(weights, v, preferred_element_type=jnp.float32)

    def attend(q):
        attend_half(source_z(q), core, kv_own, q)
        wait_sibling(KV, q)
        attend_half(source_z(q), 1 - core, kv_sib, q)

    def attend_step(m, carry):
        pl.when(m <= H)(lambda: pass_on(KV, m, 0, 1))
        pl.when(m <= H + 1)(lambda: pass_on(KV, m - 1, 1))
        pl.when(m == min(2, H))(lambda: pass_on(W_OUT, 1))
        if H == 4:
            pl.when(m == H - 1)(lambda: pass_on(W_OUT, 2))
            pl.when(m == H + 1)(lambda: pass_on(W_OUT, 3))
        pl.when(m < H)(lambda: y_pushes(Z_OUT, m + 1))
        pl.when((m >= 3) & (m <= H + 1))(lambda: y_takes(Z_OUT, m - 1))
        for_slots(m - 2, attend)
        pl.when(m >= 3)(lambda: far_takes(Z_OUT, m - 2))
        return carry

    lax.fori_loop(2, H + 3, attend_step, 0)
    for h in range(HEADS_HERE):
        at = pl.ds(h * tokens, tokens)
        mixed_ref[:, h * HD : (h + 1) * HD] = (
            o_ref[at, :] / jnp.sum(sum_ref[at, :], axis=1, keepdims=True)
        ).astype(jnp.bfloat16)

    def rs_copy(q, d):
        u = (t + d) % NT
        return pltpu.make_async_remote_copy(
            src_ref=rs_send.at[q, u],
            dst_ref=rs_recv.at[q, d - 1],
            send_sem=rs_send_sem,
            recv_sem=rs_recv_sem.at[q],
            device_id=device(ctx, u),
        )

    def share(q):
        wait_sibling(W_OUT, q)
        z_wait_sibling(Z_OUT, q)
        for i, (c, ref) in enumerate(((core, w_out_own), (1 - core, w_out_sib))):
            n = qcols // 2
            right = ref[q].reshape(half_c, n)
            part = lax.dot_general(mixed_ref[:, :n], right, NT_DIMS, preferred_element_type=jnp.float32)
            right = z_out[q, pl.ds(c * (NY // 2), NY // 2)].reshape(half_c, n)
            part += lax.dot_general(mixed_ref[:, n:], right, NT_DIMS, preferred_element_type=jnp.float32)
            part = part.astype(jnp.bfloat16).reshape(NT, rows, half_c)
            rs_send[q, :, :, i * half_c : (i + 1) * half_c] = part
        for d in range(1, NT):
            rs_copy(q, d).start()

    def add_up(q):
        whole = rs_recv.at[q]
        pltpu.make_async_copy(whole, whole, rs_recv_sem.at[q]).wait()
        total = rs_send[q, t].astype(jnp.float32)
        for d in range(1, NT):
            total += rs_recv[q, d - 1].astype(jnp.float32)
        total = total.astype(jnp.bfloat16)
        for i, c in enumerate((core, 1 - core)):
            cols = pl.ds(pl.multiple_of((source_z(q) * 2 + c) * half_c, half_c), half_c)
            out_ref[:, cols] = total[:, i * half_c : (i + 1) * half_c]

    def share_step(s, carry):
        pl.when(s == 2)(lambda: pass_on(W_OUT, H))
        for_slots(s - 1, share)

        @pl.when(s > 2)
        def _():
            for_slots(s - 3, add_up)

        return carry

    lax.fori_loop(1, H + 1, share_step, 0)
    share(H)

    def add_step(s, carry):
        for_slots(s, add_up)
        return carry

    lax.fori_loop(max(H - 2, 0), H + 1, add_step, 0)

    finish_plane(W_KV, w_in_ref)
    finish_plane(W_Q, w_in_ref)
    finish_plane(W_OUT, w_out_first)
    finish_plane(KV, kv_stage)
    for g in range(GATHERS):
        finish_gather(g)
    for g in range(Z_GATHERS):
        z_finish(g)
    for d in range(1, NT):
        norm_copy(d).wait_send()
    pltpu.make_async_copy(rs_recv, rs_recv, rs_send_sem).wait()


def per_device(NC, NT, NY, hidden_rows, norm_gain, w_qkv, w_out, doc_lengths, span_order):
    J = NY * CORES // 2
    NZ = NC // (NY * CORES)
    rows, D = hidden_rows.shape
    tokens = rows * NT
    k_rows, in_cols = w_qkv.shape
    out_rows, c_cols = w_out.shape
    qcols = HEADS_HERE * HD
    freq = THETA ** (-(np.arange(HD // 2, dtype=np.float64) * 2.0 / HD))
    freq = jnp.asarray(np.tile(freq, 2)[None, :].astype(np.float32))
    bf16, f32 = jnp.bfloat16, jnp.float32
    vmem = pl.BlockSpec(memory_space=pltpu.VMEM)
    smem = pl.BlockSpec(memory_space=pltpu.SMEM)
    hbm = pl.BlockSpec(memory_space=pltpu.HBM)
    DMA = pltpu.SemaphoreType.DMA
    return pl.pallas_call(
        functools.partial(kernel, NZ, NY, NT),
        out_shape=jax.ShapeDtypeStruct((rows, D), bf16),
        in_specs=[smem, smem, hbm, hbm, hbm, hbm, hbm],
        out_specs=vmem,
        scratch_shapes=[
            pltpu.VMEM((rows, D), bf16),
            pltpu.VMEM((D,), bf16),
            pltpu.VMEM((1, HD), f32),
            pltpu.VMEM((tokens, HD), f32),
            pltpu.VMEM((tokens, HD), f32),
            pltpu.VMEM((NZ, NY, CORES * k_rows, HD), bf16),
            pltpu.VMEM((NZ, NY, CORES * k_rows, HD), bf16),
            pltpu.VMEM((NZ, NY, CORES * k_rows, qcols // 2), bf16),
            pltpu.VMEM((NZ, NY, CORES * k_rows, qcols // 2), bf16),
            pltpu.VMEM((NZ, NY, tokens, 2 * HD), bf16),
            pltpu.VMEM((NZ, NY, tokens, 2 * HD), bf16),
            pltpu.VMEM((NZ, J, c_cols, out_rows // 2), bf16),
            pltpu.VMEM((NZ, J, c_cols, out_rows // 2), bf16),
            pltpu.VMEM((NZ, NY, CORES, c_cols, out_rows // 2), bf16),
            pltpu.VMEM((NT, rows, D), bf16),
            pltpu.VMEM((CORES, tokens, HD), f32),
            pltpu.VMEM((CORES, tokens, qcols // 2), f32),
            pltpu.VMEM((HEADS_HERE * tokens, HD), bf16),
            pltpu.VMEM((tokens, 2 * HD), bf16),
            pltpu.VMEM((HEADS_HERE * tokens, HD), f32),
            pltpu.VMEM((HEADS_HERE * tokens, HD), f32),
            pltpu.VMEM((HEADS_HERE * tokens, HD), f32),
            pltpu.VMEM((tokens, qcols), bf16),
            pltpu.VMEM((NZ, NT, rows, 2 * J * c_cols), bf16),
            pltpu.VMEM((NZ, NT - 1, rows, 2 * J * c_cols), bf16),
            DMA((GATHERS, NZ, J)),
            DMA((GATHERS, NZ)),
            DMA((GATHERS, 2 * NY)),
            DMA((GATHERS,)),
            DMA((GATHERS,)),
            DMA((NT - 1,)),
            DMA((NT,)),
            DMA,
            DMA((NZ,)),
            DMA((3,)),
            DMA((Z_GATHERS, NZ)),
            DMA((Z_GATHERS, NZ, NY)),
            DMA((Z_GATHERS, NZ)),
            DMA((Z_GATHERS,)),
            DMA((Z_GATHERS,)),
            DMA((Z_GATHERS,)),
            DMA((Z_GATHERS,)),
        ],
        compiler_params=pltpu.CompilerParams(
            collective_id=0, has_side_effects=True, vmem_limit_bytes=62 * 2**20
        ),
        cost_estimate=pl.CostEstimate(
            flops=2 * tokens * (D * in_cols + qcols * 2 * NC * tokens + out_rows * D),
            bytes_accessed=4 * rows * D,
            transcendentals=HEADS_HERE * tokens * tokens * NC,
        ),
    )(span_order, doc_lengths, hidden_rows, norm_gain, freq, w_qkv, w_out.T)


def build(mesh, NY):
    placed = (
        P(("context", "tensor"), None),
        P(),
        P("context", "tensor"),
        P("tensor", "context"),
        P(),
        P(),
    )
    return jax.shard_map(
        functools.partial(per_device, mesh.shape["context"], mesh.shape["tensor"], NY),
        mesh=mesh,
        in_specs=placed,
        out_specs=P(("context", "tensor"), None),
        check_vma=False,
    )


def solution(mesh):
    return build(mesh, Y_HI)
```
